768 devices in a mesh: comp: 8 (over y_hi, core), tile: 96 (over y_lo, x, z).
Axes of the slice: x: 4, y: 8 (y_hi: 4, y_lo: 2; y = y_hi * 2 + y_lo), z: 12, core: 2. Of those that a mesh axis runs over, the one named last changes fastest.
Arguments:
- state: float32 [8, 2, 48, 1536, 256], P('comp', None, None, 'tile'), may hold values from -6 to 6
- kappa: float32 [8, 1536, 256], P('comp', 'tile'), may hold values from 0.05 to 0.22
- forcing: float32 [8, 12, 1536, 256], P('comp', None, 'tile'), may hold values from -6 to 6
- flux_gain: float32 [8, 12], P('comp'), may hold values from -4 to 4
- src_index: int32 [8, 96, 5, 256], P('comp', 'tile'), may hold values from 0 to 4095
- intersection: float32 [8, 96, 5, 256], P('comp', 'tile'), may hold values from 0.1 to 1
- pair_count: int32 [8, 96, 5], P('comp', 'tile'), may hold values from 1 to 256, 640 in all within a row
- dst_index: int32 [8, 96, 5, 256], P('comp', 'tile'), may hold values from 0 to 4095
- cell_area: float32 [8, 1536, 256], P('comp', 'tile'), may hold values from 0.5 to 2
Outputs:
- state_out: float32 [8, 2, 48, 1536, 256], P('comp', None, None, 'tile')
- remapped: float32 [8, 12, 1536, 256], P('comp', None, 'tile')
The draws below stay inside these ranges and needn't reach their ends.
Inputs may be any that keep to these rules, and one draw needn't show every extreme that they name: `pair_count`: for every sending device the counts over its 5 partner blocks sum to 640, and one of them is exactly 256.
All inputs are finite; a program needn't handle non-finite values.
Results may differ from the reference program's by a relative error of at most 0.0029.
Values may be sent and summed in bfloat16 or wider, within the bound.
A program may use at most 32 MiB of HBM per device.

```python
import math
import jax
import jax.numpy as jnp
import numpy as np
from jax import lax

NF = 12
VARS = 2
LEV = 48
ROWS = 16
COLS = 256
NB = 5
SLOTS = 256
CELLS = 4096
NR = 1536
PAIRS_DEV = 640
N_COMP = 8
N_TILE = 96


def place_ends(drawn, rng, low, largest):
    shape = drawn.shape
    place = [jax.random.randint(jax.random.fold_in(rng, axis), (), 0, shape[axis]) for axis in range(len(shape))]
    drawn = drawn.at[tuple(place)].set(low)
    longest = shape.index(max(shape))
    place[longest] = (place[longest] + 1) % shape[longest]
    return drawn.at[tuple(place)].set(largest)


def level_of(stream_key, shape, pieces, low, top_value):
    level = 1.0
    for dim, parts in pieces:
        steps = jax.random.uniform(jax.random.fold_in(jax.random.fold_in(stream_key, 6), dim), (parts,), jnp.float32, low / len(pieces), top_value / len(pieces))
        level = level * jnp.repeat(jnp.exp(steps), shape[dim] // parts).reshape((-1,) + (1,) * (len(shape) - 1 - dim))
    return level


def length_profile(count, total, most, slope):
    weights = [(1 << 20) // math.isqrt(rank ** slope) + 1 for rank in range(2, count + 1)]
    spare, holding = total - most - (count - 1), [1] * (count - 1)
    while spare > 0:
        movable = [i for i in range(count - 1) if holding[i] < most]
        whole, budget = sum([weights[i] for i in movable]), spare
        for i in movable:
            addition = min(most - holding[i], max(1, budget * weights[i] // whole), spare)
            holding[i] = holding[i] + addition
            spare = spare - addition
    return np.array([most] + holding)


def uneven_parts(key, amount, total, reach, skew):
    if amount == 2:
        one = jax.random.randint(key, (), max(1, total - reach), min(reach, total - 1) + 1)
        return jnp.stack([one, total - one])
    tallies = jnp.asarray(length_profile(amount, total, reach, skew), jnp.int32)
    couples = (amount - 1) // 2
    donor, sink = tallies[1:1 + 2 * couples:2], tallies[2:2 + 2 * couples:2]
    margin = jnp.minimum(donor - 1, reach - sink)
    passed = jax.random.randint(jax.random.fold_in(key, 1), (couples,), 0, 1 << 20) % (margin + 1)
    tallies = tallies.at[1:1 + 2 * couples:2].set(donor - passed).at[2:2 + 2 * couples:2].set(sink + passed)
    return tallies[jax.random.permutation(jax.random.fold_in(key, 2), amount)]


def centred(key, shape, scale, most, pieces=(), held_as=jnp.bfloat16):
    array = scale * jax.random.normal(key, shape, jnp.float32)
    if pieces:
        array = array * level_of(key, shape, pieces, -0.22, 0.18)
    return jnp.clip(array, -most, most).astype(held_as)


def setup_inputs(seed: int = 0) -> dict:
    splits = jax.random.split(jax.random.key(seed), 10)
    return {
        "state": centred(splits[0], (N_COMP, VARS, LEV, NR, COLS), 1.0, 6.0, ((0, 8), (3, 96)), jnp.float32),
        "kappa": jnp.clip(0.05 + 0.17 * jax.random.uniform(splits[1], (N_COMP, NR, COLS), jnp.float32) ** level_of(splits[1], (N_COMP, NR, COLS), ((0, 8), (1, 96)), -0.2, 0.2), 0.05, 0.22),
        "forcing": centred(splits[2], (N_COMP, NF, NR, COLS), 1.0, 6.0, ((0, 8), (2, 96)), jnp.float32),
        "flux_gain": centred(splits[3], (N_COMP, NF), 1.0, 4.0, ((0, 8),), jnp.float32),
        "src_index": place_ends(jax.random.randint(splits[4], (N_COMP, N_TILE, NB, SLOTS), 0, CELLS), jax.random.fold_in(splits[4], 1), 0, CELLS - 1).astype(jnp.int32),
        "intersection": jnp.clip(jnp.exp(math.log(1.0) - 2.3025851 * jax.random.uniform(splits[5], (N_COMP, N_TILE, NB, SLOTS), jnp.float32) ** level_of(splits[5], (N_COMP, N_TILE, NB, SLOTS), ((0, 8), (1, 96)), -0.2, 0.2)), 0.1, 1.0),
        "pair_count": jax.vmap(lambda own: uneven_parts(own, NB, PAIRS_DEV, SLOTS, 2))(jax.random.split(splits[6], N_COMP * N_TILE)).reshape((N_COMP, N_TILE, NB)).astype(jnp.int32),
        "dst_index": place_ends(jax.random.randint(splits[7], (N_COMP, N_TILE, NB, SLOTS), 0, CELLS), jax.random.fold_in(splits[7], 1), 0, CELLS - 1).astype(jnp.int32),
        "cell_area": jnp.clip(jnp.exp(math.log(2.0) - 1.3862944 * jax.random.uniform(splits[8], (N_COMP, NR, COLS), jnp.float32) ** level_of(splits[8], (N_COMP, NR, COLS), ((0, 8), (1, 96)), -0.2, 0.2)), 0.5, 2.0),
    }


def dynamics(fields, kappa):
    coef = kappa[:, None, None]
    for step in range(2):
        upper = jnp.roll(fields, -1, axis=3)
        lower = jnp.roll(fields, 1, axis=3)
        right = jnp.roll(fields, -1, axis=4)
        left = jnp.roll(fields, 1, axis=4)
        lap = upper + lower + right + left - 4.0 * fields
        fields = fields + coef * lap
    return fields


def reference(state, kappa, forcing, flux_gain, src_index, intersection, pair_count, dst_index, cell_area):
    groups = state.shape[0]
    blocks = N_TILE
    state_out = dynamics(state, kappa)
    surface = state[:, :, 0]
    chosen = jnp.tile(surface, (1, NF // 2, 1, 1))
    flux = forcing + flux_gain[:, :, None, None] * chosen
    flux_dev = flux.reshape(groups, NF, blocks, CELLS).transpose(0, 2, 1, 3)
    index = src_index.reshape(groups, blocks, 1, NB * SLOTS)
    index = jnp.broadcast_to(index, (groups, blocks, NF, NB * SLOTS))
    picked = jnp.take_along_axis(flux_dev, index, axis=3).reshape(groups, blocks, NF, NB, SLOTS)
    live = jnp.arange(SLOTS, dtype=jnp.int32)[None, None, None, :] < pair_count[:, :, :, None]
    weight = jnp.where(live, intersection, jnp.float32(0.0))
    term = (weight[:, :, None, :, :] * picked).astype(jnp.bfloat16)
    term = lax.optimization_barrier(term).astype(jnp.float32)
    partner = jnp.bitwise_xor(jnp.arange(groups, dtype=jnp.int32), groups // 2)
    crossed = term[partner]
    rolled = []
    for entry in range(NB):
        offset = entry - NB // 2
        rolled.append(jnp.roll(crossed[:, :, :, entry], offset, axis=1))
    arrived = jnp.stack(rolled, axis=2).transpose(0, 1, 2, 4, 3)
    group_ids = jnp.arange(groups, dtype=jnp.int32)[:, None, None, None]
    block_ids = jnp.arange(blocks, dtype=jnp.int32)[None, :, None, None]
    global_index = (group_ids * blocks + block_ids) * CELLS + dst_index
    total = jnp.zeros((groups * blocks * CELLS, NF), jnp.float32)
    total = total.at[global_index.reshape(-1)].add(arrived.reshape(-1, NF))
    total = total.reshape(groups, blocks, ROWS, COLS, NF).transpose(0, 4, 1, 2, 3)
    remapped = total.reshape(groups, NF, blocks * ROWS, COLS) / cell_area[:, None]
    return state_out, remapped
```

```python
import functools

import jax
import jax.numpy as jnp
from jax import lax
from jax.experimental import pallas as pl
from jax.experimental.pallas import tpu as pltpu
from jax.sharding import PartitionSpec as P

MESH = pl.DeviceIdType.MESH
GROUP = 8
CHUNKS = 4
SLAB = 16


def shift_cols(x, by):
    return pltpu.roll(x, by % x.shape[-1], x.ndim - 1)


def sides(x):
    return shift_cols(x, 1) + shift_cols(x, -1)


def wide(ref, at):
    return jnp.concatenate([ref[0, at, :], ref[1, at, :]], axis=-1)


def put(ref, at, value):
    half = ref.shape[-1]
    ref[0, at, :] = value[:, :half]
    ref[1, at, :] = value[:, half:]


def one_hot(index, count):
    where = lax.broadcasted_iota(jnp.int32, (count, index.shape[1]), 0)
    return jnp.where(where == index, jnp.float32(1.0), jnp.float32(0.0))


def interior_step(low, high, coef, first, last):
    low_up = jnp.where(last, pltpu.roll(high, 7, 1), pltpu.roll(low, 7, 1))
    high_up = jnp.where(last, 0.0, pltpu.roll(high, 7, 1))
    low_down = jnp.where(first, 0.0, pltpu.roll(low, 1, 1))
    high_down = jnp.where(first, pltpu.roll(low, 1, 1), pltpu.roll(high, 1, 1))
    new_low = low + coef[0] * (low_up + low_down + sides(low) - 4.0 * low)
    new_high = high + coef[1] * (high_up + high_down + sides(high) - 4.0 * high)
    return new_low, new_high


def kernel(
    n_comp, n_tile, nvars, nf, entries, slots,
    state, kappa, forcing, gain, src, inter, count, dst, area,
    out, rem,
    field, result, surface, force, coef, cell, src_v, inter_v, dst_v, total,
    edge_out, edge_in, term_out, term_in, spread,
    load_sem, chunk_sem, edge_send, edge_recv, term_send, term_recv, store_sem,
):
    comp, tile = lax.axis_index("comp"), lax.axis_index("tile")
    partner = lax.rem(comp + n_comp // 2, n_comp)
    rows, cols = coef.shape
    levels = field.shape[1] // rows
    lanes = field.shape[2]
    below = (comp, lax.rem(tile + n_tile - 1, n_tile))
    above = (comp, lax.rem(tile + 1, n_tile))
    others = [(partner, lax.rem(tile + n_tile + j - entries // 2, n_tile)) for j in range(entries)]

    barrier = pltpu.get_barrier_semaphore()
    for device in [below, above] + others:
        pl.semaphore_signal(barrier, inc=1, device_id=device, device_id_type=MESH)

    size = field.shape[1] // CHUNKS
    per_var = field.shape[1] // nvars
    loads = [(src, src_v), (inter, inter_v)]
    loads += [(state.at[pl.ds(i * per_var, rows)], surface.at[pl.ds(i * rows, rows)]) for i in range(nvars)]
    loads += [(forcing, force)]
    n_first = len(loads)
    loads += [(kappa, coef), (dst, dst_v), (area, cell)]
    loads = [pltpu.make_async_copy(a, b, load_sem.at[i]) for i, (a, b) in enumerate(loads)]
    chunks = [
        pltpu.make_async_copy(
            state.at[pl.ds(i * size, size), pl.ds(h * lanes, lanes)], field.at[h, pl.ds(i * size, size)], chunk_sem.at[i, h]
        )
        for i in range(CHUNKS)
        for h in range(2)
    ]
    for copy in loads[:n_first] + chunks + loads[n_first:]:
        copy.start()

    for copy in loads[n_first:] + chunks:
        copy.wait()
    for side, (near, far) in enumerate(((0, 1), (rows - 1, rows - 2))):
        edge_out[side, 0:levels, :] = wide(field, pl.ds(near, levels, stride=rows)).astype(jnp.bfloat16)
        edge_out[side, levels:2 * levels, :] = wide(field, pl.ds(far, levels, stride=rows)).astype(jnp.bfloat16)
        edge_out[side, 2 * levels:, :] = jnp.broadcast_to(coef[near:near + 1, :], (16, cols)).astype(jnp.bfloat16)

    pl.semaphore_wait(barrier, 2 + entries)
    edges = [
        pltpu.make_async_remote_copy(
            src_ref=edge_out.at[side], dst_ref=edge_in.at[side], send_sem=edge_send.at[side], recv_sem=edge_recv.at[side],
            device_id=device, device_id_type=MESH,
        )
        for side, device in enumerate((below, above))
    ]
    for copy in edges:
        copy.start()

    for copy in loads[:n_first]:
        copy.wait()
    flux = [
        force[i * rows:(i + 1) * rows, :] + gain[0, i] * surface[(i % nvars) * rows:(i % nvars + 1) * rows, :]
        for i in range(nf)
    ]
    head = [x.astype(jnp.bfloat16) for x in flux]
    tail = [(x - y.astype(jnp.float32)).astype(jnp.bfloat16) for x, y in zip(flux, head, strict=True)]
    both = jnp.concatenate(head + tail, axis=0)
    slot = lax.broadcasted_iota(jnp.int32, (1, slots), 1)
    terms = []
    for j in range(entries):
        index = src_v[j]
        column = one_hot(lax.rem(index, cols), cols).astype(jnp.bfloat16)
        weight = jnp.where(slot < count[0, j], inter_v[j], 0.0)
        pick = one_hot(lax.div(index, cols), rows) * weight
        found = jnp.dot(both, column, preferred_element_type=jnp.float32)
        found = found[:nf * rows] + found[nf * rows:]
        picked = jnp.sum(found.reshape(nf, rows, slots) * pick[None], axis=1)
        term_out[j, :, :] = jnp.concatenate(
            [picked, jnp.zeros((term_out.shape[1] - nf, slots), jnp.float32)], axis=0
        ).astype(jnp.bfloat16)
        copy = pltpu.make_async_remote_copy(
            src_ref=term_out.at[j], dst_ref=term_in.at[j], send_sem=term_send.at[j], recv_sem=term_recv.at[j],
            device_id=others[j], device_id_type=MESH,
        )
        copy.start()
        terms.append(copy)

    row = lax.broadcasted_iota(jnp.int32, (GROUP, 8, cols), 1)
    first, last = row == 0, row == 7
    halves = (coef[0:8, :][None], coef[8:16, :][None])

    def group(i, carry):
        at = pl.multiple_of(i * (GROUP * rows), GROUP * rows)
        block = wide(field, pl.ds(at, GROUP * rows)).reshape(GROUP, rows, cols)
        low, high = block[:, 0:8], block[:, 8:16]
        low, high = interior_step(low, high, halves, first, last)
        low, high = interior_step(low, high, halves, first, last)
        put(result, pl.ds(at, GROUP * rows), jnp.concatenate([low, high], axis=1).reshape(GROUP * rows, cols))
        return carry

    lax.fori_loop(0, levels // GROUP, group, 0)

    for j in range(entries):
        spread[:, j * slots:(j + 1) * slots] = one_hot(lax.rem(dst_v[j], cols), cols).astype(jnp.bfloat16)
    inverse = 1.0 / cell[...]

    acc = jnp.zeros((nf * rows, cols), jnp.float32)
    for j in range(entries):
        terms[j].wait()
        here = one_hot(lax.div(dst_v[j], cols), rows)
        value = term_in[j].astype(jnp.float32)
        placed = jnp.concatenate([value[i:i + 1, :] * here for i in range(nf)], axis=0).astype(jnp.bfloat16)
        acc = acc + lax.dot_general(
            placed, spread[:, j * slots:(j + 1) * slots], (((1,), (1,)), ((), ())), preferred_element_type=jnp.float32
        )
    for i in range(nf):
        total[i * rows:(i + 1) * rows, :] = acc[i * rows:(i + 1) * rows, :] * inverse
    stores = [pltpu.make_async_copy(total, rem, store_sem.at[0])]
    stores[0].start()

    for copy in edges:
        copy.wait()
    for side, (near, far) in ((1, (0, 1)), (0, (rows - 1, rows - 2))):
        k_near, k_far = coef[near:near + 1, :], coef[far:far + 1, :]
        k_out = edge_in[side, 2 * levels:, :].astype(jnp.float32)[0:1, :]
        for g in range(0, levels, SLAB):
            h = edge_in[side, g:g + SLAB, :].astype(jnp.float32)
            h2 = edge_in[side, levels + g:levels + g + SLAB, :].astype(jnp.float32)
            at_near = pl.ds(near + g * rows, SLAB, stride=rows)
            at_far = pl.ds(far + g * rows, SLAB, stride=rows)
            a = h + k_out * (h2 + sides(h) - 4.0 * h + wide(field, at_near))
            b = k_near * h
            put(result, at_near, wide(result, at_near) + (b + k_near * (a + sides(b) - 4.0 * b)))
            put(result, at_far, wide(result, at_far) + k_far * b)
    for h in range(2):
        copy = pltpu.make_async_copy(result.at[h], out.at[:, pl.ds(h * lanes, lanes)], store_sem.at[1 + h])
        copy.start()
        stores.append(copy)
    for copy in stores:
        copy.wait()


def local(state, kappa, forcing, flux_gain, src_index, intersection, pair_count, dst_index, cell_area):
    _, nvars, deep, rows, cols = state.shape
    nf = forcing.shape[1]
    entries, slots = src_index.shape[2:]
    levels = nvars * deep
    n_comp, n_tile = lax.axis_size("comp"), lax.axis_size("tile")
    hbm = pl.BlockSpec(memory_space=pl.ANY)
    smem = pl.BlockSpec(memory_space=pltpu.SMEM)
    pad = -(-nf // 16) * 16
    f32, bf16, i32 = jnp.float32, jnp.bfloat16, jnp.int32
    dma = pltpu.SemaphoreType.DMA
    n_loads = nvars + 6
    out, rem = pl.pallas_call(
        functools.partial(kernel, n_comp, n_tile, nvars, nf, entries, slots),
        out_shape=(
            jax.ShapeDtypeStruct((levels * rows, cols), f32),
            jax.ShapeDtypeStruct((nf * rows, cols), f32),
        ),
        in_specs=[hbm, hbm, hbm, smem, hbm, hbm, smem, hbm, hbm],
        out_specs=(hbm, hbm),
        scratch_shapes=[
            pltpu.VMEM((2, levels * rows, cols // 2), f32),
            pltpu.VMEM((2, levels * rows, cols // 2), f32),
            pltpu.VMEM((nvars * rows, cols), f32),
            pltpu.VMEM((nf * rows, cols), f32),
            pltpu.VMEM((rows, cols), f32),
            pltpu.VMEM((rows, cols), f32),
            pltpu.VMEM((entries, 1, slots), i32),
            pltpu.VMEM((entries, 1, slots), f32),
            pltpu.VMEM((entries, 1, slots), i32),
            pltpu.VMEM((nf * rows, cols), f32),
            pltpu.VMEM((2, 2 * levels + 16, cols), bf16),
            pltpu.VMEM((2, 2 * levels + 16, cols), bf16),
            pltpu.VMEM((entries, pad, slots), bf16),
            pltpu.VMEM((entries, pad, slots), bf16),
            pltpu.VMEM((cols, entries * slots), bf16),
            dma((n_loads,)),
            dma((CHUNKS, 2)),
            dma((2,)),
            dma((2,)),
            dma((entries,)),
            dma((entries,)),
            dma((3,)),
        ],
        compiler_params=pltpu.CompilerParams(
            collective_id=0, has_side_effects=True, vmem_limit_bytes=56 * 1024 * 1024
        ),
        cost_estimate=pl.CostEstimate(flops=10**8, bytes_accessed=4 * 10**6, transcendentals=0),
    )(
        state.reshape(levels * rows, cols),
        kappa[0],
        forcing.reshape(nf * rows, cols),
        flux_gain,
        src_index.reshape(entries, 1, slots),
        intersection.reshape(entries, 1, slots),
        pair_count.reshape(1, entries),
        dst_index.reshape(entries, 1, slots),
        cell_area[0],
    )
    return out.reshape(1, nvars, deep, rows, cols), rem.reshape(1, nf, rows, cols)


def solution(mesh):
    return jax.shard_map(
        local,
        mesh=mesh,
        in_specs=(
            P("comp", None, None, "tile", None),
            P("comp", "tile", None),
            P("comp", None, "tile", None),
            P("comp", None),
            P("comp", "tile", None, None),
            P("comp", "tile", None, None),
            P("comp", "tile", None),
            P("comp", "tile", None, None),
            P("comp", "tile", None),
        ),
        out_specs=(P("comp", None, None, "tile", None), P("comp", None, "tile", None)),
        check_vma=False,
    )
```

```python
import functools

import jax
import jax.numpy as jnp
from jax import lax
from jax.experimental import pallas as pl
from jax.experimental.pallas import tpu as pltpu
from jax.sharding import PartitionSpec as P

MESH = pl.DeviceIdType.MESH
GROUP = 8
CHUNKS = 4
SLAB = 16
LIMIT = 40 * 1024 * 1024


def shift_cols(x, by):
    return pltpu.roll(x, by % x.shape[-1], x.ndim - 1)


def sides(x):
    return shift_cols(x, 1) + shift_cols(x, -1)


def wide(ref, at):
    return jnp.concatenate([ref[0, at, :], ref[1, at, :]], axis=-1)


def put(ref, at, value):
    half = ref.shape[-1]
    ref[0, at, :] = value[:, :half]
    ref[1, at, :] = value[:, half:]


def one_hot(index, count):
    where = lax.broadcasted_iota(jnp.int32, (count, index.shape[1]), 0)
    return jnp.where(where == index, jnp.float32(1.0), jnp.float32(0.0))


def interior_step(low, high, coef, first, last):
    low_up = jnp.where(last, pltpu.roll(high, 7, 1), pltpu.roll(low, 7, 1))
    high_up = jnp.where(last, 0.0, pltpu.roll(high, 7, 1))
    low_down = jnp.where(first, 0.0, pltpu.roll(low, 1, 1))
    high_down = jnp.where(first, pltpu.roll(low, 1, 1), pltpu.roll(high, 1, 1))
    new_low = low + coef[0] * (low_up + low_down + sides(low) - 4.0 * low)
    new_high = high + coef[1] * (high_up + high_down + sides(high) - 4.0 * high)
    return new_low, new_high


def kernel(
    n_comp, n_tile, nvars, nf, entries, slots,
    state, kappa, forcing, gain, src, inter, count, dst, area,
    result, term_in, spread, masks, inverse,
    field, surface, force, coef, cell, src_v, inter_v, dst_v,
    edge_out, edge_in, term_out,
    load_sem, chunk_sem, edge_send, edge_recv, term_send, term_recv,
):
    comp, tile = lax.axis_index("comp"), lax.axis_index("tile")
    partner = lax.rem(comp + n_comp // 2, n_comp)
    rows, cols = coef.shape
    levels = field.shape[1] // rows
    lanes = field.shape[2]
    below = (comp, lax.rem(tile + n_tile - 1, n_tile))
    above = (comp, lax.rem(tile + 1, n_tile))
    others = [(partner, lax.rem(tile + n_tile + j - entries // 2, n_tile)) for j in range(entries)]

    barrier = pltpu.get_barrier_semaphore()
    for device in [below, above] + others:
        pl.semaphore_signal(barrier, inc=1, device_id=device, device_id_type=MESH)

    size = field.shape[1] // CHUNKS
    per_var = field.shape[1] // nvars
    loads = [(src, src_v), (inter, inter_v)]
    loads += [(state.at[pl.ds(i * per_var, rows)], surface.at[pl.ds(i * rows, rows)]) for i in range(nvars)]
    loads += [(forcing, force)]
    n_first = len(loads)
    loads += [(kappa, coef), (dst, dst_v), (area, cell)]
    loads = [pltpu.make_async_copy(a, b, load_sem.at[i]) for i, (a, b) in enumerate(loads)]
    chunks = [
        pltpu.make_async_copy(
            state.at[pl.ds(i * size, size), pl.ds(h * lanes, lanes)], field.at[h, pl.ds(i * size, size)], chunk_sem.at[i, h]
        )
        for i in range(CHUNKS)
        for h in range(2)
    ]
    for copy in loads[:n_first] + chunks + loads[n_first:]:
        copy.start()

    for copy in loads[n_first:] + chunks:
        copy.wait()
    for side, (near, far) in enumerate(((0, 1), (rows - 1, rows - 2))):
        edge_out[side, 0:levels, :] = wide(field, pl.ds(near, levels, stride=rows)).astype(jnp.bfloat16)
        edge_out[side, levels:2 * levels, :] = wide(field, pl.ds(far, levels, stride=rows)).astype(jnp.bfloat16)
        edge_out[side, 2 * levels:, :] = jnp.broadcast_to(coef[near:near + 1, :], (16, cols)).astype(jnp.bfloat16)

    pl.semaphore_wait(barrier, 2 + entries)
    edges = [
        pltpu.make_async_remote_copy(
            src_ref=edge_out.at[side], dst_ref=edge_in.at[side], send_sem=edge_send.at[side], recv_sem=edge_recv.at[side],
            device_id=device, device_id_type=MESH,
        )
        for side, device in enumerate((below, above))
    ]
    for copy in edges:
        copy.start()

    for copy in loads[:n_first]:
        copy.wait()
    flux = [
        force[i * rows:(i + 1) * rows, :] + gain[0, i] * surface[(i % nvars) * rows:(i % nvars + 1) * rows, :]
        for i in range(nf)
    ]
    head = [x.astype(jnp.bfloat16) for x in flux]
    tail = [(x - y.astype(jnp.float32)).astype(jnp.bfloat16) for x, y in zip(flux, head, strict=True)]
    both = jnp.concatenate(head + tail, axis=0)
    slot = lax.broadcasted_iota(jnp.int32, (1, slots), 1)
    terms = []
    for j in range(entries):
        index = src_v[j]
        column = one_hot(lax.rem(index, cols), cols).astype(jnp.bfloat16)
        weight = jnp.where(slot < count[0, j], inter_v[j], 0.0)
        pick = one_hot(lax.div(index, cols), rows) * weight
        found = jnp.dot(both, column, preferred_element_type=jnp.float32)
        found = found[:nf * rows] + found[nf * rows:]
        picked = jnp.sum(found.reshape(nf, rows, slots) * pick[None], axis=1)
        term_out[j, :, :] = jnp.concatenate(
            [picked, jnp.zeros((term_out.shape[1] - nf, slots), jnp.float32)], axis=0
        ).astype(jnp.bfloat16)
        copy = pltpu.make_async_remote_copy(
            src_ref=term_out.at[j], dst_ref=term_in.at[j], send_sem=term_send.at[j], recv_sem=term_recv.at[j],
            device_id=others[j], device_id_type=MESH,
        )
        copy.start()
        terms.append(copy)

    row = lax.broadcasted_iota(jnp.int32, (GROUP, 8, cols), 1)
    first, last = row == 0, row == 7
    halves = (coef[0:8, :][None], coef[8:16, :][None])

    def group(i, carry):
        at = pl.multiple_of(i * (GROUP * rows), GROUP * rows)
        block = wide(field, pl.ds(at, GROUP * rows)).reshape(GROUP, rows, cols)
        low, high = block[:, 0:8], block[:, 8:16]
        low, high = interior_step(low, high, halves, first, last)
        low, high = interior_step(low, high, halves, first, last)
        put(result, pl.ds(at, GROUP * rows), jnp.concatenate([low, high], axis=1).reshape(GROUP * rows, cols))
        return carry

    lax.fori_loop(0, levels // GROUP, group, 0)

    for j in range(entries):
        spread[j * slots:(j + 1) * slots, :] = one_hot(lax.rem(dst_v[j], cols), cols).T.astype(jnp.bfloat16)
        masks[j, :, :] = one_hot(lax.div(dst_v[j], cols), rows)
    inverse[...] = 1.0 / cell[...]

    for copy in edges:
        copy.wait()
    for side, (near, far) in ((1, (0, 1)), (0, (rows - 1, rows - 2))):
        k_near, k_far = coef[near:near + 1, :], coef[far:far + 1, :]
        k_out = edge_in[side, 2 * levels:, :].astype(jnp.float32)[0:1, :]
        for g in range(0, levels, SLAB):
            h = edge_in[side, g:g + SLAB, :].astype(jnp.float32)
            h2 = edge_in[side, levels + g:levels + g + SLAB, :].astype(jnp.float32)
            at_near = pl.ds(near + g * rows, SLAB, stride=rows)
            at_far = pl.ds(far + g * rows, SLAB, stride=rows)
            a = h + k_out * (h2 + sides(h) - 4.0 * h + wide(field, at_near))
            b = k_near * h
            put(result, at_near, wide(result, at_near) + (b + k_near * (a + sides(b) - 4.0 * b)))
            put(result, at_far, wide(result, at_far) + k_far * b)
    for copy in terms:
        copy.wait()


def finish_kernel(nvars, nf, entries, slots, result, term_in, spread, masks, inverse, out, rem, total, store_sem):
    lanes = result.shape[2]
    rows, cols = inverse.shape
    stores = [
        pltpu.make_async_copy(result.at[h], out.at[:, pl.ds(h * lanes, lanes)], store_sem.at[h]) for h in range(2)
    ]
    for copy in stores:
        copy.start()
    placed = []
    for j in range(entries):
        value = term_in[j].astype(jnp.float32)
        here = masks[j]
        placed.append(jnp.concatenate([value[i:i + 1, :] * here for i in range(nf)], axis=0).astype(jnp.bfloat16))
    acc = jnp.dot(jnp.concatenate(placed, axis=1), spread[...], preferred_element_type=jnp.float32)
    scale = inverse[...]
    for i in range(nf):
        total[i * rows:(i + 1) * rows, :] = acc[i * rows:(i + 1) * rows, :] * scale
    stores.append(pltpu.make_async_copy(total, rem, store_sem.at[2]))
    stores[-1].start()
    for copy in stores:
        copy.wait()


def local(state, kappa, forcing, flux_gain, src_index, intersection, pair_count, dst_index, cell_area):
    _, nvars, deep, rows, cols = state.shape
    nf = forcing.shape[1]
    entries, slots = src_index.shape[2:]
    levels = nvars * deep
    n_comp, n_tile = lax.axis_size("comp"), lax.axis_size("tile")
    hbm = pl.BlockSpec(memory_space=pl.ANY)
    smem = pl.BlockSpec(memory_space=pltpu.SMEM)
    pad = -(-nf // 16) * 16
    f32, bf16, i32 = jnp.float32, jnp.bfloat16, jnp.int32
    dma = pltpu.SemaphoreType.DMA
    n_loads = nvars + 6
    vmem = pl.BlockSpec(memory_space=pltpu.VMEM)
    passed = pl.pallas_call(
        functools.partial(kernel, n_comp, n_tile, nvars, nf, entries, slots),
        out_shape=(
            pltpu.VMEM((2, levels * rows, cols // 2), f32),
            pltpu.VMEM((entries, pad, slots), bf16),
            pltpu.VMEM((entries * slots, cols), bf16),
            pltpu.VMEM((entries, rows, slots), f32),
            pltpu.VMEM((rows, cols), f32),
        ),
        in_specs=[hbm, hbm, hbm, smem, hbm, hbm, smem, hbm, hbm],
        out_specs=(vmem,) * 5,
        scratch_shapes=[
            pltpu.VMEM((2, levels * rows, cols // 2), f32),
            pltpu.VMEM((nvars * rows, cols), f32),
            pltpu.VMEM((nf * rows, cols), f32),
            pltpu.VMEM((rows, cols), f32),
            pltpu.VMEM((rows, cols), f32),
            pltpu.VMEM((entries, 1, slots), i32),
            pltpu.VMEM((entries, 1, slots), f32),
            pltpu.VMEM((entries, 1, slots), i32),
            pltpu.VMEM((2, 2 * levels + 16, cols), bf16),
            pltpu.VMEM((2, 2 * levels + 16, cols), bf16),
            pltpu.VMEM((entries, pad, slots), bf16),
            dma((n_loads,)),
            dma((CHUNKS, 2)),
            dma((2,)),
            dma((2,)),
            dma((entries,)),
            dma((entries,)),
        ],
        compiler_params=pltpu.CompilerParams(
            collective_id=0, has_side_effects=True, vmem_limit_bytes=LIMIT
        ),
        cost_estimate=pl.CostEstimate(flops=10**8, bytes_accessed=4 * 10**6, transcendentals=0),
    )(
        *[
            pltpu.with_memory_space_constraint(x, pltpu.HBM)
            for x in (
                state.reshape(levels * rows, cols),
                kappa[0],
                forcing.reshape(nf * rows, cols),
                flux_gain,
                src_index.reshape(entries, 1, slots),
                intersection.reshape(entries, 1, slots),
                pair_count.reshape(1, entries),
                dst_index.reshape(entries, 1, slots),
                cell_area[0],
            )
        ]
    )
    out, rem = pl.pallas_call(
        functools.partial(finish_kernel, nvars, nf, entries, slots),
        out_shape=(
            jax.ShapeDtypeStruct((levels * rows, cols), f32),
            jax.ShapeDtypeStruct((nf * rows, cols), f32),
        ),
        in_specs=[vmem] * 5,
        out_specs=(hbm, hbm),
        scratch_shapes=[pltpu.VMEM((nf * rows, cols), f32), dma((3,))],
        compiler_params=pltpu.CompilerParams(vmem_limit_bytes=LIMIT),
        cost_estimate=pl.CostEstimate(flops=10**8, bytes_accessed=4 * 10**6, transcendentals=0),
    )(*passed)
    return out.reshape(1, nvars, deep, rows, cols), rem.reshape(1, nf, rows, cols)


def solution(mesh):
    return jax.shard_map(
        local,
        mesh=mesh,
        in_specs=(
            P("comp", None, None, "tile", None),
            P("comp", "tile", None),
            P("comp", None, "tile", None),
            P("comp", None),
            P("comp", "tile", None, None),
            P("comp", "tile", None, None),
            P("comp", "tile", None),
            P("comp", "tile", None, None),
            P("comp", "tile", None),
        ),
        out_specs=(P("comp", None, None, "tile", None), P("comp", None, "tile", None)),
        check_vma=False,
    )
```

```python
import functools

import jax
import jax.numpy as jnp
from jax import lax
from jax.experimental import pallas as pl
from jax.experimental.pallas import tpu as pltpu
from jax.sharding import PartitionSpec as P

MESH = pl.DeviceIdType.MESH
GROUP = 8
CHUNKS = 4
SLAB = 16
DEPTH = 12
LIMIT = 40 * 1024 * 1024


def shift_cols(x, by):
    return pltpu.roll(x, by % x.shape[-1], x.ndim - 1)


def sides(x):
    return shift_cols(x, 1) + shift_cols(x, -1)


def wide(ref, at):
    return jnp.concatenate([ref[0, at, :], ref[1, at, :]], axis=-1)


def put(ref, at, value):
    half = ref.shape[-1]
    ref[0, at, :] = value[:, :half]
    ref[1, at, :] = value[:, half:]


def one_hot(index, count):
    where = lax.broadcasted_iota(jnp.int32, (count, index.shape[1]), 0)
    return jnp.where(where == index, jnp.float32(1.0), jnp.float32(0.0))


def interior_step(low, high, coef, first, last):
    low_up = jnp.where(last, pltpu.roll(high, 7, 1), pltpu.roll(low, 7, 1))
    high_up = jnp.where(last, 0.0, pltpu.roll(high, 7, 1))
    low_down = jnp.where(first, 0.0, pltpu.roll(low, 1, 1))
    high_down = jnp.where(first, pltpu.roll(low, 1, 1), pltpu.roll(high, 1, 1))
    new_low = low + coef[0] * (low_up + low_down + sides(low) - 4.0 * low)
    new_high = high + coef[1] * (high_up + high_down + sides(high) - 4.0 * high)
    return new_low, new_high


def kernel(
    n_comp, n_tile, nvars, nf, entries, slots,
    state, kappa, forcing, gain, src, inter, count, dst, area,
    result, term_in, spread, masks, inverse,
    field, surface, force, coef, cell, src_v, inter_v, dst_v, gain_s, count_s,
    edge_out, edge_in, term_out,
    ready, load_sem, edge_send, edge_recv, term_send, term_recv,
):
    comp, tile = lax.axis_index("comp"), lax.axis_index("tile")
    partner = lax.rem(comp + n_comp // 2, n_comp)
    rows, cols = coef.shape
    levels = field.shape[1] // rows
    lanes = field.shape[2]
    shift = cols.bit_length() - 1
    below = (comp, lax.rem(tile + n_tile - 1, n_tile))
    above = (comp, lax.rem(tile + 1, n_tile))
    others = [(partner, lax.rem(tile + n_tile + j - entries // 2, n_tile)) for j in range(entries)]

    half = n_tile // 2
    deep = min(DEPTH, half)
    wide_by = half // deep
    x, z, y = lax.rem(lax.div(tile, deep), wide_by), lax.rem(tile, deep), 2 * lax.div(comp, 2) + lax.div(tile, half)

    def rank(offset, across):
        over, under = z + offset >= deep, z + offset < 0
        z_there = z + offset + jnp.where(under, deep, 0) - jnp.where(over, deep, 0)
        x_there = x + jnp.where(over, 1, 0) - jnp.where(under, 1, 0)
        turn = jnp.logical_or(x_there == wide_by, x_there < 0)
        x_there = jnp.where(turn, jnp.where(over, 0, wide_by - 1), x_there)
        y_there = jnp.where(turn, y + 1 - 2 * lax.rem(y, 2), y)
        if across:
            y_there = lax.rem(y_there + n_comp // 2, n_comp)
        when = 13 * jnp.minimum(z_there, 7) + 4 * jnp.maximum(z_there - 7, 0) + 4 * x_there
        when = when + jnp.where(y_there < 4, 6 * y_there, 42 - 3 * y_there)
        to_tile = lax.rem(tile + n_tile + offset, n_tile)
        return (when * n_comp + (partner if across else comp)) * n_tile + to_tile

    own = rank(0, False)

    def after(offset, across):
        return rank(offset, across) > own

    peers = {}
    for j in range(entries):
        offset = j - entries // 2
        peers["term", offset] = (others[j], after(offset, True), j, entries - 1 - j, j)
    peers["edge", -1] = (below, after(-1, False), 0, 1, entries)
    peers["edge", 1] = (above, after(1, False), 1, 0, entries + 1)
    order = [("term", 0), ("edge", 1), ("term", 1), ("term", 2), ("edge", -1), ("term", -2), ("term", -1)]

    sends = [("term", 1), ("term", 2), ("term", -2), ("term", -1), ("term", 0), ("edge", 1), ("edge", -1)]
    barrier = pltpu.get_barrier_semaphore()
    before = 0
    for key in order:
        device, is_after = peers[key][:2]

        @pl.when(is_after)
        def _(device=device):
            pl.semaphore_signal(barrier, inc=1, device_id=device, device_id_type=MESH)

        before = before + jnp.where(is_after, 0, 1)

    size = field.shape[1] // CHUNKS
    per_var = field.shape[1] // nvars
    early = [(src, src_v), (gain, gain_s), (count, count_s), (inter, inter_v)]
    early += [(state.at[pl.ds(i * per_var, rows)], surface.at[pl.ds(i * rows, rows)]) for i in range(nvars)]
    early += [(forcing, force)]
    middle = [(kappa, coef)] + [
        (state.at[pl.ds(i * size, size), pl.ds(h * lanes, lanes)], field.at[h, pl.ds(i * size, size)])
        for i in range(CHUNKS)
        for h in range(2)
    ]
    late = [(dst, dst_v), (area, cell)]
    copies = [pltpu.make_async_copy(a, b, load_sem.at[i]) for i, (a, b) in enumerate(early + middle + late)]
    early, middle, late = copies[:len(early)], copies[len(early):len(early) + len(middle)], copies[-len(late):]
    for copy in copies:
        copy.start()

    @pl.when(before > 0)
    def _():
        pl.semaphore_wait(barrier, before)

    for key in sends:
        device, is_after, _, _, number = peers[key]

        @pl.when(jnp.logical_not(is_after))
        def _(device=device, number=number):
            pl.semaphore_signal(ready.at[number], inc=1, device_id=device, device_id_type=MESH)

    for copy in early:
        copy.wait()
    flux = [
        force[i * rows:(i + 1) * rows, :] + gain_s[0, i] * surface[(i % nvars) * rows:(i % nvars + 1) * rows, :]
        for i in range(nf)
    ]
    head = [x.astype(jnp.bfloat16) for x in flux]
    tail = [(x - y.astype(jnp.float32)).astype(jnp.bfloat16) for x, y in zip(flux, head, strict=True)]
    both = jnp.concatenate([jnp.concatenate(head, axis=0), jnp.concatenate(tail, axis=0)], axis=1)
    slot = lax.broadcasted_iota(jnp.int32, (1, slots), 1)
    for j in range(entries):
        index = src_v[j]
        column = one_hot(index & (cols - 1), cols).astype(jnp.bfloat16)
        weight = jnp.where(slot < count_s[0, j], inter_v[j], 0.0)
        pick = one_hot(index >> shift, rows) * weight
        found = jnp.dot(both, jnp.concatenate([column, column], axis=0), preferred_element_type=jnp.float32)
        picked = jnp.sum(found.reshape(nf, rows, slots) * pick[None], axis=1)
        term_out[j, :, :] = jnp.concatenate(
            [picked, jnp.zeros((term_out.shape[1] - nf, slots), jnp.float32)], axis=0
        ).astype(jnp.bfloat16)

    def to(key):
        device, _, out_slot = peers[key][:3]
        here, there, done, came = (
            (term_out, term_in, term_send, term_recv) if key[0] == "term" else (edge_out, edge_in, edge_send, edge_recv)
        )
        return pltpu.make_async_remote_copy(
            src_ref=here.at[out_slot], dst_ref=there.at[out_slot], send_sem=done.at[out_slot], recv_sem=came.at[out_slot],
            device_id=device, device_id_type=MESH,
        )

    def arrived(key):
        slot_in = peers[key][3]
        there, done, came = (term_in, term_send, term_recv) if key[0] == "term" else (edge_in, edge_send, edge_recv)
        pltpu.make_async_remote_copy(
            src_ref=there.at[slot_in], dst_ref=there.at[slot_in], send_sem=done.at[slot_in], recv_sem=came.at[slot_in],
            device_id=peers[key][0], device_id_type=MESH,
        ).wait_recv()

    for key in sends[:entries]:

        @pl.when(jnp.logical_not(peers[key][1]))
        def _(key=key):
            to(key).start()

    for copy in middle:
        copy.wait()
    for side, (near, far) in enumerate(((0, 1), (rows - 1, rows - 2))):
        edge_out[side, 0:levels, :] = wide(field, pl.ds(near, levels, stride=rows)).astype(jnp.bfloat16)
        edge_out[side, levels:2 * levels, :] = wide(field, pl.ds(far, levels, stride=rows)).astype(jnp.bfloat16)
        edge_out[side, 2 * levels:, :] = jnp.broadcast_to(coef[near:near + 1, :], (16, cols)).astype(jnp.bfloat16)

    for key in sends[entries:]:

        @pl.when(jnp.logical_not(peers[key][1]))
        def _(key=key):
            to(key).start()

    row = lax.broadcasted_iota(jnp.int32, (GROUP, 8, cols), 1)
    first, last = row == 0, row == 7
    halves = (coef[0:8, :][None], coef[8:16, :][None])

    def group(i, carry):
        at = pl.multiple_of(i * (GROUP * rows), GROUP * rows)
        block = wide(field, pl.ds(at, GROUP * rows)).reshape(GROUP, rows, cols)
        low, high = block[:, 0:8], block[:, 8:16]
        low, high = interior_step(low, high, halves, first, last)
        low, high = interior_step(low, high, halves, first, last)
        put(result, pl.ds(at, GROUP * rows), jnp.concatenate([low, high], axis=1).reshape(GROUP * rows, cols))
        return carry

    lax.fori_loop(0, levels // GROUP, group, 0)

    for copy in late:
        copy.wait()
    for j in range(entries):
        spread[j * slots:(j + 1) * slots, :] = one_hot(dst_v[j] & (cols - 1), cols).T.astype(jnp.bfloat16)
        masks[j, :, :] = one_hot(dst_v[j] >> shift, rows)
    inverse[...] = 1.0 / cell[...]

    for key in order:

        @pl.when(peers[key][1])
        def _(key=key):
            kind, offset = key
            pl.semaphore_wait(ready.at[peers[kind, -offset][4]], 1)
            to(key).start()

    arrived(("edge", 1))
    arrived(("edge", -1))
    for side, (near, far) in ((1, (0, 1)), (0, (rows - 1, rows - 2))):
        k_near, k_far = coef[near:near + 1, :], coef[far:far + 1, :]
        k_out = edge_in[side, 2 * levels:, :].astype(jnp.float32)[0:1, :]
        for g in range(0, levels, SLAB):
            h = edge_in[side, g:g + SLAB, :].astype(jnp.float32)
            h2 = edge_in[side, levels + g:levels + g + SLAB, :].astype(jnp.float32)
            at_near = pl.ds(near + g * rows, SLAB, stride=rows)
            at_far = pl.ds(far + g * rows, SLAB, stride=rows)
            a = h + k_out * (h2 + sides(h) - 4.0 * h + wide(field, at_near))
            b = k_near * h
            put(result, at_near, wide(result, at_near) + (b + k_near * (a + sides(b) - 4.0 * b)))
            put(result, at_far, wide(result, at_far) + k_far * b)
    for key in order:
        if key[0] == "term":
            arrived(key)
    for key in order:
        to(key).wait_send()


def finish_kernel(nvars, nf, entries, slots, result, term_in, spread, masks, inverse, out, rem, total, store_sem):
    lanes = result.shape[2]
    rows, cols = inverse.shape
    stores = [
        pltpu.make_async_copy(result.at[h], out.at[:, pl.ds(h * lanes, lanes)], store_sem.at[h]) for h in range(2)
    ]
    for copy in stores:
        copy.start()
    placed = []
    for j in range(entries):
        value = term_in[j].astype(jnp.float32)
        here = masks[j]
        placed.append(jnp.concatenate([value[i:i + 1, :] * here for i in range(nf)], axis=0).astype(jnp.bfloat16))
    acc = jnp.dot(jnp.concatenate(placed, axis=1), spread[...], preferred_element_type=jnp.float32)
    scale = inverse[...]
    for i in range(nf):
        total[i * rows:(i + 1) * rows, :] = acc[i * rows:(i + 1) * rows, :] * scale
    stores.append(pltpu.make_async_copy(total, rem, store_sem.at[2]))
    stores[-1].start()
    for copy in stores:
        copy.wait()


def local(state, kappa, forcing, flux_gain, src_index, intersection, pair_count, dst_index, cell_area):
    _, nvars, deep, rows, cols = state.shape
    nf = forcing.shape[1]
    entries, slots = src_index.shape[2:]
    levels = nvars * deep
    n_comp, n_tile = lax.axis_size("comp"), lax.axis_size("tile")
    hbm = pl.BlockSpec(memory_space=pl.ANY)
    pad = -(-nf // 16) * 16
    f32, bf16, i32 = jnp.float32, jnp.bfloat16, jnp.int32
    dma = pltpu.SemaphoreType.DMA
    n_loads = nvars + 8 + 2 * CHUNKS
    vmem = pl.BlockSpec(memory_space=pltpu.VMEM)
    passed = pl.pallas_call(
        functools.partial(kernel, n_comp, n_tile, nvars, nf, entries, slots),
        out_shape=(
            pltpu.VMEM((2, levels * rows, cols // 2), f32),
            pltpu.VMEM((entries, pad, slots), bf16),
            pltpu.VMEM((entries * slots, cols), bf16),
            pltpu.VMEM((entries, rows, slots), f32),
            pltpu.VMEM((rows, cols), f32),
        ),
        in_specs=[hbm] * 9,
        out_specs=(vmem,) * 5,
        scratch_shapes=[
            pltpu.VMEM((2, levels * rows, cols // 2), f32),
            pltpu.VMEM((nvars * rows, cols), f32),
            pltpu.VMEM((nf * rows, cols), f32),
            pltpu.VMEM((rows, cols), f32),
            pltpu.VMEM((rows, cols), f32),
            pltpu.VMEM((entries, 1, slots), i32),
            pltpu.VMEM((entries, 1, slots), f32),
            pltpu.VMEM((entries, 1, slots), i32),
            pltpu.SMEM((1, nf), f32),
            pltpu.SMEM((1, entries), i32),
            pltpu.VMEM((2, 2 * levels + 16, cols), bf16),
            pltpu.VMEM((2, 2 * levels + 16, cols), bf16),
            pltpu.VMEM((entries, pad, slots), bf16),
            pltpu.SemaphoreType.REGULAR((entries + 2,)),
            dma((n_loads,)),
            dma((2,)),
            dma((2,)),
            dma((entries,)),
            dma((entries,)),
        ],
        compiler_params=pltpu.CompilerParams(
            collective_id=0, has_side_effects=True, vmem_limit_bytes=LIMIT
        ),
        cost_estimate=pl.CostEstimate(flops=10**8, bytes_accessed=4 * 10**6, transcendentals=0),
    )(
        *[
            pltpu.with_memory_space_constraint(x, pltpu.HBM)
            for x in (
                state.reshape(levels * rows, cols),
                kappa[0],
                forcing.reshape(nf * rows, cols),
                flux_gain,
                src_index.reshape(entries, 1, slots),
                intersection.reshape(entries, 1, slots),
                pair_count.reshape(1, entries),
                dst_index.reshape(entries, 1, slots),
                cell_area[0],
            )
        ]
    )
    out, rem = pl.pallas_call(
        functools.partial(finish_kernel, nvars, nf, entries, slots),
        out_shape=(
            jax.ShapeDtypeStruct((levels * rows, cols), f32),
            jax.ShapeDtypeStruct((nf * rows, cols), f32),
        ),
        in_specs=[vmem] * 5,
        out_specs=(hbm, hbm),
        scratch_shapes=[pltpu.VMEM((nf * rows, cols), f32), dma((3,))],
        compiler_params=pltpu.CompilerParams(vmem_limit_bytes=LIMIT),
        cost_estimate=pl.CostEstimate(flops=10**8, bytes_accessed=4 * 10**6, transcendentals=0),
    )(*passed)
    return out.reshape(1, nvars, deep, rows, cols), rem.reshape(1, nf, rows, cols)


def solution(mesh):
    return jax.shard_map(
        local,
        mesh=mesh,
        in_specs=(
            P("comp", None, None, "tile", None),
            P("comp", "tile", None),
            P("comp", None, "tile", None),
            P("comp", None),
            P("comp", "tile", None, None),
            P("comp", "tile", None, None),
            P("comp", "tile", None),
            P("comp", "tile", None, None),
            P("comp", "tile", None),
        ),
        out_specs=(P("comp", None, None, "tile", None), P("comp", None, "tile", None)),
        check_vma=False,
    )
```

```python
import functools

import jax
import jax.numpy as jnp
from jax import lax
from jax.experimental import pallas as pl
from jax.experimental.pallas import tpu as pltpu
from jax.sharding import PartitionSpec as P

MESH = pl.DeviceIdType.MESH
GROUP = 8
CHUNKS = 1
SLAB = 16
DEPTH = 12
LIMIT = 40 * 1024 * 1024


def shift_cols(x, by):
    return pltpu.roll(x, by % x.shape[-1], x.ndim - 1)


def sides(x):
    return shift_cols(x, 1) + shift_cols(x, -1)


def wide(ref, at):
    return jnp.concatenate([ref[0, at, :], ref[1, at, :]], axis=-1)


def put(ref, at, value):
    half = ref.shape[-1]
    ref[0, at, :] = value[:, :half]
    ref[1, at, :] = value[:, half:]


def wrapped(i, n):
    return jnp.where(i < 0, i + n, jnp.where(i >= n, i - n, i))


def one_hot(index, count):
    where = lax.broadcasted_iota(jnp.int32, (count, index.shape[1]), 0)
    return jnp.where(where == index, jnp.float32(1.0), jnp.float32(0.0))


def interior_step(low, high, coef, first, last):
    low_up = jnp.where(last, pltpu.roll(high, 7, 1), pltpu.roll(low, 7, 1))
    high_up = jnp.where(last, 0.0, pltpu.roll(high, 7, 1))
    low_down = jnp.where(first, 0.0, pltpu.roll(low, 1, 1))
    high_down = jnp.where(first, pltpu.roll(low, 1, 1), pltpu.roll(high, 1, 1))
    new_low = low + coef[0] * (low_up + low_down + sides(low) - 4.0 * low)
    new_high = high + coef[1] * (high_up + high_down + sides(high) - 4.0 * high)
    return new_low, new_high


def kernel(
    n_comp, n_tile, nvars, nf, entries, slots,
    state, kappa, forcing, gain, src, inter, count, dst, area,
    result, term_in, spread, masks, inverse,
    field, surface, force, coef, cell, src_v, inter_v, dst_v, gain_s, count_s,
    edge_out, edge_in, term_out,
    ready, load_sem, edge_send, edge_recv, term_send, term_recv,
):
    comp, tile = lax.axis_index("comp"), lax.axis_index("tile")
    partner = jnp.where(comp < n_comp // 2, comp + n_comp // 2, comp - n_comp // 2)
    rows, cols = coef.shape
    levels = field.shape[1] // rows
    lanes = field.shape[2]
    shift = cols.bit_length() - 1
    reach = entries // 2
    tiles = {o: wrapped(tile + o, n_tile) for o in range(-reach, reach + 1)}
    below, above = (comp, tiles[-1]), (comp, tiles[1])
    others = [(partner, tiles[j - reach]) for j in range(entries)]

    size = field.shape[1] // CHUNKS
    per_var = field.shape[1] // nvars
    early = [(src, src_v), (gain, gain_s), (count, count_s), (inter, inter_v)]
    early += [(state.at[pl.ds(i * per_var, rows)], surface.at[pl.ds(i * rows, rows)]) for i in range(nvars)]
    early += [(forcing, force)]
    middle = [(kappa, coef)] + [
        (state.at[pl.ds(i * size, size), pl.ds(h * lanes, lanes)], field.at[h, pl.ds(i * size, size)])
        for i in range(CHUNKS)
        for h in range(2)
    ]
    late = [(dst, dst_v), (area, cell)]
    copies = [pltpu.make_async_copy(a, b, load_sem.at[i]) for i, (a, b) in enumerate(early + middle + late)]
    early, middle, late = copies[:len(early)], copies[len(early):len(early) + len(middle)], copies[-len(late):]
    for copy in copies:
        copy.start()

    half = n_tile // 2
    deep = min(DEPTH, half)
    wide_by = half // deep
    y_low = jnp.where(tile >= half, 1, 0)
    rest = tile - half * y_low
    x = sum(jnp.where(rest >= deep * i, 1, 0) for i in range(1, wide_by)) if wide_by > 1 else 0
    z = rest - deep * x
    y_high = comp >> 1
    y_across = partner >> 1

    def rank(offset, across):
        over, under = z + offset >= deep, z + offset < 0
        z_there = wrapped(z + offset, deep)
        x_there = x + jnp.where(over, 1, 0) - jnp.where(under, 1, 0)
        turn = jnp.logical_or(x_there >= wide_by, x_there < 0)
        x_there = wrapped(x_there, wide_by)
        y_there = 2 * (y_across if across else y_high) + jnp.where(turn, 1 - y_low, y_low)
        when = 4 * z_there + 9 * jnp.minimum(z_there, 7) + 4 * x_there
        when = when + jnp.where(y_there < 4, 6 * y_there, 42 - 3 * y_there)
        return (when * n_comp + (partner if across else comp)) * n_tile + tiles[offset]

    own = rank(0, False)

    def after(offset, across):
        return rank(offset, across) > own

    peers = {}
    for j in range(entries):
        offset = j - entries // 2
        peers["term", offset] = (others[j], after(offset, True), j, entries - 1 - j, j)
    peers["edge", -1] = (below, after(-1, False), 0, 1, entries)
    peers["edge", 1] = (above, after(1, False), 1, 0, entries + 1)
    order = [("term", 0), ("edge", 1), ("term", 1), ("term", 2), ("edge", -1), ("term", -2), ("term", -1)]

    sends = [("term", 1), ("term", 2), ("term", -2), ("term", -1), ("term", 0), ("edge", 1), ("edge", -1)]
    barrier = pltpu.get_barrier_semaphore()
    before = 0
    for key in order:
        device, is_after = peers[key][:2]

        @pl.when(is_after)
        def _(device=device):
            pl.semaphore_signal(barrier, inc=1, device_id=device, device_id_type=MESH)

        before = before + jnp.where(is_after, 0, 1)

    @pl.when(before > 0)
    def _():
        pl.semaphore_wait(barrier, before)

    for key in sends:
        device, is_after, _, _, number = peers[key]

        @pl.when(jnp.logical_not(is_after))
        def _(device=device, number=number):
            pl.semaphore_signal(ready.at[number], inc=1, device_id=device, device_id_type=MESH)

    for copy in early:
        copy.wait()
    flux = [
        force[i * rows:(i + 1) * rows, :] + gain_s[0, i] * surface[(i % nvars) * rows:(i % nvars + 1) * rows, :]
        for i in range(nf)
    ]
    head = [x.astype(jnp.bfloat16) for x in flux]
    tail = [(x - y.astype(jnp.float32)).astype(jnp.bfloat16) for x, y in zip(flux, head, strict=True)]
    both = jnp.concatenate([jnp.concatenate(head, axis=0), jnp.concatenate(tail, axis=0)], axis=1)
    def to(key):
        device, _, out_slot = peers[key][:3]
        here, there, done, came = (
            (term_out, term_in, term_send, term_recv) if key[0] == "term" else (edge_out, edge_in, edge_send, edge_recv)
        )
        return pltpu.make_async_remote_copy(
            src_ref=here.at[out_slot], dst_ref=there.at[out_slot], send_sem=done.at[out_slot], recv_sem=came.at[out_slot],
            device_id=device, device_id_type=MESH,
        )

    def arrived(key):
        slot_in = peers[key][3]
        there, done, came = (term_in, term_send, term_recv) if key[0] == "term" else (edge_in, edge_send, edge_recv)
        pltpu.make_async_remote_copy(
            src_ref=there.at[slot_in], dst_ref=there.at[slot_in], send_sem=done.at[slot_in], recv_sem=came.at[slot_in],
            device_id=peers[key][0], device_id_type=MESH,
        ).wait_recv()

    slot = lax.broadcasted_iota(jnp.int32, (1, slots), 1)
    def compute(j):
        index = src_v[j]
        column = one_hot(index & (cols - 1), cols).astype(jnp.bfloat16)
        weight = jnp.where(slot < count_s[0, j], inter_v[j], 0.0)
        pick = one_hot(index >> shift, rows) * weight
        found = jnp.dot(both, jnp.concatenate([column, column], axis=0), preferred_element_type=jnp.float32)
        picked = jnp.sum(found.reshape(nf, rows, slots) * pick[None], axis=1)
        term_out[j, :, :] = jnp.concatenate(
            [picked, jnp.zeros((term_out.shape[1] - nf, slots), jnp.float32)], axis=0
        ).astype(jnp.bfloat16)

    for group in (sends[:2], sends[2:entries]):
        for key in group:
            compute(peers[key][2])
        for key in group:

            @pl.when(jnp.logical_not(peers[key][1]))
            def _(key=key):
                to(key).start()

    for copy in middle:
        copy.wait()
    for side, (near, far) in enumerate(((0, 1), (rows - 1, rows - 2))):
        edge_out[side, 0:levels, :] = wide(field, pl.ds(near, levels, stride=rows)).astype(jnp.bfloat16)
        edge_out[side, levels:2 * levels, :] = wide(field, pl.ds(far, levels, stride=rows)).astype(jnp.bfloat16)
        edge_out[side, 2 * levels:, :] = jnp.broadcast_to(coef[near:near + 1, :], (16, cols)).astype(jnp.bfloat16)

    for key in sends[entries:]:

        @pl.when(jnp.logical_not(peers[key][1]))
        def _(key=key):
            to(key).start()

    row = lax.broadcasted_iota(jnp.int32, (GROUP, 8, cols), 1)
    first, last = row == 0, row == 7
    halves = (coef[0:8, :][None], coef[8:16, :][None])

    def group(i, carry):
        at = pl.multiple_of(i * (GROUP * rows), GROUP * rows)
        block = wide(field, pl.ds(at, GROUP * rows)).reshape(GROUP, rows, cols)
        low, high = block[:, 0:8], block[:, 8:16]
        low, high = interior_step(low, high, halves, first, last)
        low, high = interior_step(low, high, halves, first, last)
        put(result, pl.ds(at, GROUP * rows), jnp.concatenate([low, high], axis=1).reshape(GROUP * rows, cols))
        return carry

    lax.fori_loop(0, levels // GROUP, group, 0)

    for copy in late:
        copy.wait()
    for j in range(entries):
        spread[j * slots:(j + 1) * slots, :] = one_hot(dst_v[j] & (cols - 1), cols).T.astype(jnp.bfloat16)
        masks[j, :, :] = one_hot(dst_v[j] >> shift, rows)
    inverse[...] = 1.0 / cell[...]

    near = [("term", -2), ("term", -1), ("edge", -1), ("edge", 1), ("term", 0), ("term", 1), ("term", 2)]
    for wraps, keys in ((False, near), (True, [("edge", -1), ("term", -2), ("term", -1)])):
        for key in keys:
            kind, offset = key
            due = peers[key][1]
            if offset < 0:
                under = z + offset < 0
                due = jnp.logical_and(due, under if wraps else jnp.logical_not(under))

            @pl.when(due)
            def _(key=key, kind=kind, offset=offset):
                pl.semaphore_wait(ready.at[peers[kind, -offset][4]], 1)
                to(key).start()

    arrived(("edge", 1))
    arrived(("edge", -1))
    for side, (near, far) in ((1, (0, 1)), (0, (rows - 1, rows - 2))):
        k_near, k_far = coef[near:near + 1, :], coef[far:far + 1, :]
        k_out = edge_in[side, 2 * levels:, :].astype(jnp.float32)[0:1, :]
        for g in range(0, levels, SLAB):
            h = edge_in[side, g:g + SLAB, :].astype(jnp.float32)
            h2 = edge_in[side, levels + g:levels + g + SLAB, :].astype(jnp.float32)
            at_near = pl.ds(near + g * rows, SLAB, stride=rows)
            at_far = pl.ds(far + g * rows, SLAB, stride=rows)
            a = h + k_out * (h2 + sides(h) - 4.0 * h + wide(field, at_near))
            b = k_near * h
            put(result, at_near, wide(result, at_near) + (b + k_near * (a + sides(b) - 4.0 * b)))
            put(result, at_far, wide(result, at_far) + k_far * b)
    for key in order:
        if key[0] == "term":
            arrived(key)
    for key in order:
        to(key).wait_send()


def finish_kernel(nvars, nf, entries, slots, result, term_in, spread, masks, inverse, out, rem, total, store_sem):
    lanes = result.shape[2]
    rows, cols = inverse.shape
    stores = [
        pltpu.make_async_copy(result.at[h], out.at[:, pl.ds(h * lanes, lanes)], store_sem.at[h]) for h in range(2)
    ]
    for copy in stores:
        copy.start()
    placed = []
    for j in range(entries):
        value = term_in[j].astype(jnp.float32)
        here = masks[j]
        placed.append(jnp.concatenate([value[i:i + 1, :] * here for i in range(nf)], axis=0).astype(jnp.bfloat16))
    acc = jnp.dot(jnp.concatenate(placed, axis=1), spread[...], preferred_element_type=jnp.float32)
    scale = inverse[...]
    for i in range(nf):
        total[i * rows:(i + 1) * rows, :] = acc[i * rows:(i + 1) * rows, :] * scale
    stores.append(pltpu.make_async_copy(total, rem, store_sem.at[2]))
    stores[-1].start()
    for copy in stores:
        copy.wait()


def local(state, kappa, forcing, flux_gain, src_index, intersection, pair_count, dst_index, cell_area):
    _, nvars, deep, rows, cols = state.shape
    nf = forcing.shape[1]
    entries, slots = src_index.shape[2:]
    levels = nvars * deep
    n_comp, n_tile = lax.axis_size("comp"), lax.axis_size("tile")
    hbm = pl.BlockSpec(memory_space=pl.ANY)
    pad = -(-nf // 16) * 16
    f32, bf16, i32 = jnp.float32, jnp.bfloat16, jnp.int32
    dma = pltpu.SemaphoreType.DMA
    n_loads = nvars + 8 + 2 * CHUNKS
    vmem = pl.BlockSpec(memory_space=pltpu.VMEM)
    passed = pl.pallas_call(
        functools.partial(kernel, n_comp, n_tile, nvars, nf, entries, slots),
        out_shape=(
            pltpu.VMEM((2, levels * rows, cols // 2), f32),
            pltpu.VMEM((entries, pad, slots), bf16),
            pltpu.VMEM((entries * slots, cols), bf16),
            pltpu.VMEM((entries, rows, slots), f32),
            pltpu.VMEM((rows, cols), f32),
        ),
        in_specs=[hbm] * 9,
        out_specs=(vmem,) * 5,
        scratch_shapes=[
            pltpu.VMEM((2, levels * rows, cols // 2), f32),
            pltpu.VMEM((nvars * rows, cols), f32),
            pltpu.VMEM((nf * rows, cols), f32),
            pltpu.VMEM((rows, cols), f32),
            pltpu.VMEM((rows, cols), f32),
            pltpu.VMEM((entries, 1, slots), i32),
            pltpu.VMEM((entries, 1, slots), f32),
            pltpu.VMEM((entries, 1, slots), i32),
            pltpu.SMEM((1, nf), f32),
            pltpu.SMEM((1, entries), i32),
            pltpu.VMEM((2, 2 * levels + 16, cols), bf16),
            pltpu.VMEM((2, 2 * levels + 16, cols), bf16),
            pltpu.VMEM((entries, pad, slots), bf16),
            pltpu.SemaphoreType.REGULAR((entries + 2,)),
            dma((n_loads,)),
            dma((2,)),
            dma((2,)),
            dma((entries,)),
            dma((entries,)),
        ],
        compiler_params=pltpu.CompilerParams(
            collective_id=0, has_side_effects=True, vmem_limit_bytes=LIMIT
        ),
        cost_estimate=pl.CostEstimate(flops=10**8, bytes_accessed=4 * 10**6, transcendentals=0),
    )(
        *[
            pltpu.with_memory_space_constraint(x, pltpu.HBM)
            for x in (
                state.reshape(levels * rows, cols),
                kappa[0],
                forcing.reshape(nf * rows, cols),
                flux_gain,
                src_index.reshape(entries, 1, slots),
                intersection.reshape(entries, 1, slots),
                pair_count.reshape(1, entries),
                dst_index.reshape(entries, 1, slots),
                cell_area[0],
            )
        ]
    )
    out, rem = pl.pallas_call(
        functools.partial(finish_kernel, nvars, nf, entries, slots),
        out_shape=(
            jax.ShapeDtypeStruct((levels * rows, cols), f32),
            jax.ShapeDtypeStruct((nf * rows, cols), f32),
        ),
        in_specs=[vmem] * 5,
        out_specs=(hbm, hbm),
        scratch_shapes=[pltpu.VMEM((nf * rows, cols), f32), dma((3,))],
        compiler_params=pltpu.CompilerParams(vmem_limit_bytes=LIMIT),
        cost_estimate=pl.CostEstimate(flops=10**8, bytes_accessed=4 * 10**6, transcendentals=0),
    )(*passed)
    return out.reshape(1, nvars, deep, rows, cols), rem.reshape(1, nf, rows, cols)


def solution(mesh):
    return jax.shard_map(
        local,
        mesh=mesh,
        in_specs=(
            P("comp", None, None, "tile", None),
            P("comp", "tile", None),
            P("comp", None, "tile", None),
            P("comp", None),
            P("comp", "tile", None, None),
            P("comp", "tile", None, None),
            P("comp", "tile", None),
            P("comp", "tile", None, None),
            P("comp", "tile", None),
        ),
        out_specs=(P("comp", None, None, "tile", None), P("comp", None, "tile", None)),
        check_vma=False,
    )
```

```python
import functools

import jax
import jax.numpy as jnp
from jax import lax
from jax.experimental import pallas as pl
from jax.experimental.pallas import tpu as pltpu
from jax.sharding import PartitionSpec as P

MESH = pl.DeviceIdType.MESH
GROUP = 8
CHUNKS = 1
SLAB = 16
DEPTH = 12
LIMIT = 40 * 1024 * 1024


def shift_cols(x, by):
    return pltpu.roll(x, by % x.shape[-1], x.ndim - 1)


def sides(x):
    return shift_cols(x, 1) + shift_cols(x, -1)


def wide(ref, at):
    return jnp.concatenate([ref[0, at, :], ref[1, at, :]], axis=-1)


def put(ref, at, value):
    half = ref.shape[-1]
    ref[0, at, :] = value[:, :half]
    ref[1, at, :] = value[:, half:]


def wrapped(i, n):
    return jnp.where(i < 0, i + n, jnp.where(i >= n, i - n, i))


def one_hot(index, count):
    where = lax.broadcasted_iota(jnp.int32, (count, index.shape[1]), 0)
    return jnp.where(where == index, jnp.float32(1.0), jnp.float32(0.0))


def interior_step(low, high, coef, first, last):
    low_up = jnp.where(last, pltpu.roll(high, 7, 1), pltpu.roll(low, 7, 1))
    high_up = jnp.where(last, 0.0, pltpu.roll(high, 7, 1))
    low_down = jnp.where(first, 0.0, pltpu.roll(low, 1, 1))
    high_down = jnp.where(first, pltpu.roll(low, 1, 1), pltpu.roll(high, 1, 1))
    new_low = low + coef[0] * (low_up + low_down + sides(low) - 4.0 * low)
    new_high = high + coef[1] * (high_up + high_down + sides(high) - 4.0 * high)
    return new_low, new_high


def kernel(
    n_comp, n_tile, nvars, nf, entries, slots,
    state, kappa, forcing, gain, src, inter, count, dst, area,
    result, term_in, spread, masks, inverse,
    field, surface, force, coef, cell, src_v, inter_v, dst_v, gain_s, count_s,
    edge_out, edge_in, term_out,
    ready, load_sem, edge_send, edge_recv, term_send, term_recv,
):
    comp, tile = lax.axis_index("comp"), lax.axis_index("tile")
    partner = jnp.where(comp < n_comp // 2, comp + n_comp // 2, comp - n_comp // 2)
    rows, cols = coef.shape
    levels = field.shape[1] // rows
    lanes = field.shape[2]
    shift = cols.bit_length() - 1
    reach = entries // 2
    tiles = {o: wrapped(tile + o, n_tile) for o in range(-reach, reach + 1)}
    below, above = (comp, tiles[-1]), (comp, tiles[1])
    others = [(partner, tiles[j - reach]) for j in range(entries)]

    size = field.shape[1] // CHUNKS
    per_var = field.shape[1] // nvars
    early = [(src, src_v), (gain, gain_s), (count, count_s), (inter, inter_v)]
    early += [(state.at[pl.ds(i * per_var, rows)], surface.at[pl.ds(i * rows, rows)]) for i in range(nvars)]
    early += [(forcing, force)]
    middle = [(kappa, coef)] + [
        (state.at[pl.ds(i * size, size), pl.ds(h * lanes, lanes)], field.at[h, pl.ds(i * size, size)])
        for i in range(CHUNKS)
        for h in range(2)
    ]
    late = [(dst, dst_v), (area, cell)]
    copies = [pltpu.make_async_copy(a, b, load_sem.at[i]) for i, (a, b) in enumerate(early + middle + late)]
    early, middle, late = copies[:len(early)], copies[len(early):len(early) + len(middle)], copies[-len(late):]
    for copy in copies:
        copy.start()

    half = n_tile // 2
    deep = min(DEPTH, half)
    wide_by = half // deep
    y_low = jnp.where(tile >= half, 1, 0)
    rest = tile - half * y_low
    x = sum(jnp.where(rest >= deep * i, 1, 0) for i in range(1, wide_by)) if wide_by > 1 else 0
    z = rest - deep * x
    y_high = comp >> 1
    y_across = partner >> 1

    def rank(offset, across):
        over, under = z + offset >= deep, z + offset < 0
        z_there = wrapped(z + offset, deep)
        x_there = x + jnp.where(over, 1, 0) - jnp.where(under, 1, 0)
        turn = jnp.logical_or(x_there >= wide_by, x_there < 0)
        x_there = wrapped(x_there, wide_by)
        y_there = 2 * (y_across if across else y_high) + jnp.where(turn, 1 - y_low, y_low)
        when = 4 * z_there + 9 * jnp.minimum(z_there, 7) + 4 * x_there
        when = when + jnp.where(y_there < 4, 6 * y_there, 54 - 3 * y_there)
        return (when * n_comp + (partner if across else comp)) * n_tile + tiles[offset]

    own = rank(0, False)

    def after(offset, across):
        return rank(offset, across) > own

    peers = {}
    for j in range(entries):
        offset = j - entries // 2
        peers["term", offset] = (others[j], after(offset, True), j, entries - 1 - j, j)
    peers["edge", -1] = (below, after(-1, False), 0, 1, entries)
    peers["edge", 1] = (above, after(1, False), 1, 0, entries + 1)
    order = [("term", 0), ("edge", 1), ("term", 1), ("term", 2), ("edge", -1), ("term", -2), ("term", -1)]

    sends = [("term", 1), ("term", 2), ("term", -2), ("term", -1), ("term", 0), ("edge", 1), ("edge", -1)]
    barrier = pltpu.get_barrier_semaphore()
    before = 0
    for key in order:
        device, is_after = peers[key][:2]

        @pl.when(is_after)
        def _(device=device):
            pl.semaphore_signal(barrier, inc=1, device_id=device, device_id_type=MESH)

        before = before + jnp.where(is_after, 0, 1)

    @pl.when(before > 0)
    def _():
        pl.semaphore_wait(barrier, before)

    for key in sends:
        device, is_after, _, _, number = peers[key]

        @pl.when(jnp.logical_not(is_after))
        def _(device=device, number=number):
            pl.semaphore_signal(ready.at[number], inc=1, device_id=device, device_id_type=MESH)

    for copy in early:
        copy.wait()
    flux = [
        force[i * rows:(i + 1) * rows, :] + gain_s[0, i] * surface[(i % nvars) * rows:(i % nvars + 1) * rows, :]
        for i in range(nf)
    ]
    head = [x.astype(jnp.bfloat16) for x in flux]
    tail = [(x - y.astype(jnp.float32)).astype(jnp.bfloat16) for x, y in zip(flux, head, strict=True)]
    both = jnp.concatenate([jnp.concatenate(head, axis=0), jnp.concatenate(tail, axis=0)], axis=1)
    def to(key):
        device, _, out_slot = peers[key][:3]
        here, there, done, came = (
            (term_out, term_in, term_send, term_recv) if key[0] == "term" else (edge_out, edge_in, edge_send, edge_recv)
        )
        return pltpu.make_async_remote_copy(
            src_ref=here.at[out_slot], dst_ref=there.at[out_slot], send_sem=done.at[out_slot], recv_sem=came.at[out_slot],
            device_id=device, device_id_type=MESH,
        )

    def arrived(key):
        slot_in = peers[key][3]
        there, done, came = (term_in, term_send, term_recv) if key[0] == "term" else (edge_in, edge_send, edge_recv)
        pltpu.make_async_remote_copy(
            src_ref=there.at[slot_in], dst_ref=there.at[slot_in], send_sem=done.at[slot_in], recv_sem=came.at[slot_in],
            device_id=peers[key][0], device_id_type=MESH,
        ).wait_recv()

    slot = lax.broadcasted_iota(jnp.int32, (1, slots), 1)
    def compute(j):
        index = src_v[j]
        column = one_hot(index & (cols - 1), cols).astype(jnp.bfloat16)
        weight = jnp.where(slot < count_s[0, j], inter_v[j], 0.0)
        pick = one_hot(index >> shift, rows) * weight
        found = jnp.dot(both, jnp.concatenate([column, column], axis=0), preferred_element_type=jnp.float32)
        picked = jnp.sum(found.reshape(nf, rows, slots) * pick[None], axis=1)
        term_out[j, :, :] = jnp.concatenate(
            [picked, jnp.zeros((term_out.shape[1] - nf, slots), jnp.float32)], axis=0
        ).astype(jnp.bfloat16)

    def leave(group):
        for key in group:
            compute(peers[key][2])
        for key in group:

            @pl.when(jnp.logical_not(peers[key][1]))
            def _(key=key):
                to(key).start()

    leave(sends[:2])
    for copy in middle:
        copy.wait()
    for side, (near, far) in enumerate(((0, 1), (rows - 1, rows - 2))):
        edge_out[side, 0:levels, :] = wide(field, pl.ds(near, levels, stride=rows)).astype(jnp.bfloat16)
        edge_out[side, levels:2 * levels, :] = wide(field, pl.ds(far, levels, stride=rows)).astype(jnp.bfloat16)
        edge_out[side, 2 * levels:, :] = jnp.broadcast_to(coef[near:near + 1, :], (16, cols)).astype(jnp.bfloat16)

    for key in sends[entries:]:

        @pl.when(jnp.logical_not(peers[key][1]))
        def _(key=key):
            to(key).start()

    leave(sends[2:entries])

    row = lax.broadcasted_iota(jnp.int32, (GROUP, 8, cols), 1)
    first, last = row == 0, row == 7
    halves = (coef[0:8, :][None], coef[8:16, :][None])

    def group(i, carry):
        at = pl.multiple_of(i * (GROUP * rows), GROUP * rows)
        block = wide(field, pl.ds(at, GROUP * rows)).reshape(GROUP, rows, cols)
        low, high = block[:, 0:8], block[:, 8:16]
        low, high = interior_step(low, high, halves, first, last)
        low, high = interior_step(low, high, halves, first, last)
        put(result, pl.ds(at, GROUP * rows), jnp.concatenate([low, high], axis=1).reshape(GROUP * rows, cols))
        return carry

    lax.fori_loop(0, levels // GROUP, group, 0)

    for copy in late:
        copy.wait()
    for j in range(entries):
        spread[j * slots:(j + 1) * slots, :] = one_hot(dst_v[j] & (cols - 1), cols).T.astype(jnp.bfloat16)
        masks[j, :, :] = one_hot(dst_v[j] >> shift, rows)
    inverse[...] = 1.0 / cell[...]

    near = [("term", -2), ("term", -1), ("edge", -1), ("edge", 1), ("term", 0), ("term", 1), ("term", 2)]
    for wraps, keys in ((False, near), (True, [("edge", -1), ("term", -2), ("term", -1)])):
        for key in keys:
            kind, offset = key
            due = peers[key][1]
            if offset < 0:
                under = z + offset < 0
                due = jnp.logical_and(due, under if wraps else jnp.logical_not(under))

            @pl.when(due)
            def _(key=key, kind=kind, offset=offset):
                pl.semaphore_wait(ready.at[peers[kind, -offset][4]], 1)
                to(key).start()

    arrived(("edge", 1))
    arrived(("edge", -1))
    for side, (near, far) in ((1, (0, 1)), (0, (rows - 1, rows - 2))):
        k_near, k_far = coef[near:near + 1, :], coef[far:far + 1, :]
        k_out = edge_in[side, 2 * levels:, :].astype(jnp.float32)[0:1, :]
        for g in range(0, levels, SLAB):
            h = edge_in[side, g:g + SLAB, :].astype(jnp.float32)
            h2 = edge_in[side, levels + g:levels + g + SLAB, :].astype(jnp.float32)
            at_near = pl.ds(near + g * rows, SLAB, stride=rows)
            at_far = pl.ds(far + g * rows, SLAB, stride=rows)
            a = h + k_out * (h2 + sides(h) - 4.0 * h + wide(field, at_near))
            b = k_near * h
            put(result, at_near, wide(result, at_near) + (b + k_near * (a + sides(b) - 4.0 * b)))
            put(result, at_far, wide(result, at_far) + k_far * b)
    for key in order:
        if key[0] == "term":
            arrived(key)
    for key in order:
        to(key).wait_send()


def finish_kernel(nvars, nf, entries, slots, result, term_in, spread, masks, inverse, out, rem, total, store_sem):
    lanes = result.shape[2]
    rows, cols = inverse.shape
    stores = [
        pltpu.make_async_copy(result.at[h], out.at[:, pl.ds(h * lanes, lanes)], store_sem.at[h]) for h in range(2)
    ]
    for copy in stores:
        copy.start()
    placed = []
    for j in range(entries):
        value = term_in[j].astype(jnp.float32)
        here = masks[j]
        placed.append(jnp.concatenate([value[i:i + 1, :] * here for i in range(nf)], axis=0).astype(jnp.bfloat16))
    acc = jnp.dot(jnp.concatenate(placed, axis=1), spread[...], preferred_element_type=jnp.float32)
    scale = inverse[...]
    for i in range(nf):
        total[i * rows:(i + 1) * rows, :] = acc[i * rows:(i + 1) * rows, :] * scale
    stores.append(pltpu.make_async_copy(total, rem, store_sem.at[2]))
    stores[-1].start()
    for copy in stores:
        copy.wait()


def local(state, kappa, forcing, flux_gain, src_index, intersection, pair_count, dst_index, cell_area):
    _, nvars, deep, rows, cols = state.shape
    nf = forcing.shape[1]
    entries, slots = src_index.shape[2:]
    levels = nvars * deep
    n_comp, n_tile = lax.axis_size("comp"), lax.axis_size("tile")
    hbm = pl.BlockSpec(memory_space=pl.ANY)
    pad = -(-nf // 16) * 16
    f32, bf16, i32 = jnp.float32, jnp.bfloat16, jnp.int32
    dma = pltpu.SemaphoreType.DMA
    n_loads = nvars + 8 + 2 * CHUNKS
    vmem = pl.BlockSpec(memory_space=pltpu.VMEM)
    passed = pl.pallas_call(
        functools.partial(kernel, n_comp, n_tile, nvars, nf, entries, slots),
        out_shape=(
            pltpu.VMEM((2, levels * rows, cols // 2), f32),
            pltpu.VMEM((entries, pad, slots), bf16),
            pltpu.VMEM((entries * slots, cols), bf16),
            pltpu.VMEM((entries, rows, slots), f32),
            pltpu.VMEM((rows, cols), f32),
        ),
        in_specs=[hbm] * 9,
        out_specs=(vmem,) * 5,
        scratch_shapes=[
            pltpu.VMEM((2, levels * rows, cols // 2), f32),
            pltpu.VMEM((nvars * rows, cols), f32),
            pltpu.VMEM((nf * rows, cols), f32),
            pltpu.VMEM((rows, cols), f32),
            pltpu.VMEM((rows, cols), f32),
            pltpu.VMEM((entries, 1, slots), i32),
            pltpu.VMEM((entries, 1, slots), f32),
            pltpu.VMEM((entries, 1, slots), i32),
            pltpu.SMEM((1, nf), f32),
            pltpu.SMEM((1, entries), i32),
            pltpu.VMEM((2, 2 * levels + 16, cols), bf16),
            pltpu.VMEM((2, 2 * levels + 16, cols), bf16),
            pltpu.VMEM((entries, pad, slots), bf16),
            pltpu.SemaphoreType.REGULAR((entries + 2,)),
            dma((n_loads,)),
            dma((2,)),
            dma((2,)),
            dma((entries,)),
            dma((entries,)),
        ],
        compiler_params=pltpu.CompilerParams(
            collective_id=0, has_side_effects=True, vmem_limit_bytes=LIMIT
        ),
        cost_estimate=pl.CostEstimate(flops=10**8, bytes_accessed=4 * 10**6, transcendentals=0),
    )(
        *[
            pltpu.with_memory_space_constraint(x, pltpu.HBM)
            for x in (
                state.reshape(levels * rows, cols),
                kappa[0],
                forcing.reshape(nf * rows, cols),
                flux_gain,
                src_index.reshape(entries, 1, slots),
                intersection.reshape(entries, 1, slots),
                pair_count.reshape(1, entries),
                dst_index.reshape(entries, 1, slots),
                cell_area[0],
            )
        ]
    )
    out, rem = pl.pallas_call(
        functools.partial(finish_kernel, nvars, nf, entries, slots),
        out_shape=(
            jax.ShapeDtypeStruct((levels * rows, cols), f32),
            jax.ShapeDtypeStruct((nf * rows, cols), f32),
        ),
        in_specs=[vmem] * 5,
        out_specs=(hbm, hbm),
        scratch_shapes=[pltpu.VMEM((nf * rows, cols), f32), dma((3,))],
        compiler_params=pltpu.CompilerParams(vmem_limit_bytes=LIMIT),
        cost_estimate=pl.CostEstimate(flops=10**8, bytes_accessed=4 * 10**6, transcendentals=0),
    )(*passed)
    return out.reshape(1, nvars, deep, rows, cols), rem.reshape(1, nf, rows, cols)


def solution(mesh):
    return jax.shard_map(
        local,
        mesh=mesh,
        in_specs=(
            P("comp", None, None, "tile", None),
            P("comp", "tile", None),
            P("comp", None, "tile", None),
            P("comp", None),
            P("comp", "tile", None, None),
            P("comp", "tile", None, None),
            P("comp", "tile", None),
            P("comp", "tile", None, None),
            P("comp", "tile", None),
        ),
        out_specs=(P("comp", None, None, "tile", None), P("comp", None, "tile", None)),
        check_vma=False,
    )
```

```python
import functools

import jax
import jax.numpy as jnp
from jax import lax
from jax.experimental import pallas as pl
from jax.experimental.pallas import tpu as pltpu
from jax.sharding import PartitionSpec as P

MESH = pl.DeviceIdType.MESH
GROUP = 8
CHUNKS = 1
SLAB = 16
DEPTH = 12
LIMIT = 40 * 1024 * 1024


def shift_cols(x, by):
    return pltpu.roll(x, by % x.shape[-1], x.ndim - 1)


def sides(x):
    return shift_cols(x, 1) + shift_cols(x, -1)


def wide(ref, at):
    return jnp.concatenate([ref[0, at, :], ref[1, at, :]], axis=-1)


def put(ref, at, value):
    half = ref.shape[-1]
    ref[0, at, :] = value[:, :half]
    ref[1, at, :] = value[:, half:]


def wrapped(i, n):
    return jnp.where(i < 0, i + n, jnp.where(i >= n, i - n, i))


def one_hot(index, count):
    where = lax.broadcasted_iota(jnp.int32, (count, index.shape[1]), 0)
    return jnp.where(where == index, jnp.float32(1.0), jnp.float32(0.0))


def interior_step(low, high, coef, first, last):
    low_up = jnp.where(last, pltpu.roll(high, 7, 1), pltpu.roll(low, 7, 1))
    high_up = jnp.where(last, 0.0, pltpu.roll(high, 7, 1))
    low_down = jnp.where(first, 0.0, pltpu.roll(low, 1, 1))
    high_down = jnp.where(first, pltpu.roll(low, 1, 1), pltpu.roll(high, 1, 1))
    new_low = low + coef[0] * (low_up + low_down + sides(low) - 4.0 * low)
    new_high = high + coef[1] * (high_up + high_down + sides(high) - 4.0 * high)
    return new_low, new_high


def kernel(
    n_comp, n_tile, nvars, nf, entries, slots,
    state, kappa, forcing, gain, src, inter, count, dst, area,
    result, term_in, spread, masks, inverse,
    field, surface, force, coef, cell, src_v, inter_v, dst_v, gain_s, count_s,
    edge_out, edge_in, term_out,
    ready, load_sem, edge_send, edge_recv, term_send, term_recv,
):
    comp, tile = lax.axis_index("comp"), lax.axis_index("tile")
    partner = jnp.where(comp < n_comp // 2, comp + n_comp // 2, comp - n_comp // 2)
    rows, cols = coef.shape
    levels = field.shape[1] // rows
    lanes = field.shape[2]
    shift = cols.bit_length() - 1
    reach = entries // 2
    tiles = {o: wrapped(tile + o, n_tile) for o in range(-reach, reach + 1)}
    below, above = (comp, tiles[-1]), (comp, tiles[1])
    others = [(partner, tiles[j - reach]) for j in range(entries)]

    size = field.shape[1] // CHUNKS
    per_var = field.shape[1] // nvars
    early = [(src, src_v), (gain, gain_s), (count, count_s), (inter, inter_v)]
    early += [(state.at[pl.ds(i * per_var, rows)], surface.at[pl.ds(i * rows, rows)]) for i in range(nvars)]
    early += [(forcing, force)]
    middle = [(kappa, coef)] + [
        (state.at[pl.ds(i * size, size), pl.ds(h * lanes, lanes)], field.at[h, pl.ds(i * size, size)])
        for i in range(CHUNKS)
        for h in range(2)
    ]
    late = [(dst, dst_v), (area, cell)]
    copies = [pltpu.make_async_copy(a, b, load_sem.at[i]) for i, (a, b) in enumerate(early + middle + late)]
    early, middle, late = copies[:len(early)], copies[len(early):len(early) + len(middle)], copies[-len(late):]
    for copy in copies:
        copy.start()

    half = n_tile // 2
    deep = min(DEPTH, half)
    wide_by = half // deep
    y_low = jnp.where(tile >= half, 1, 0)
    rest = tile - half * y_low
    x = sum(jnp.where(rest >= deep * i, 1, 0) for i in range(1, wide_by)) if wide_by > 1 else 0
    z = rest - deep * x
    y_high = comp >> 1
    y_across = partner >> 1

    def rank(offset, across):
        over, under = z + offset >= deep, z + offset < 0
        z_there = wrapped(z + offset, deep)
        x_there = x + jnp.where(over, 1, 0) - jnp.where(under, 1, 0)
        turn = jnp.logical_or(x_there >= wide_by, x_there < 0)
        x_there = wrapped(x_there, wide_by)
        y_there = 2 * (y_across if across else y_high) + jnp.where(turn, 1 - y_low, y_low)
        when = 4 * z_there + 9 * jnp.minimum(z_there, 7) + 4 * x_there
        when = when + jnp.where(y_there < 4, 6 * y_there, 54 - 3 * y_there)
        return (when * n_comp + (partner if across else comp)) * n_tile + tiles[offset]

    own = rank(0, False)

    def after(offset, across):
        return rank(offset, across) > own

    peers = {}
    for j in range(entries):
        offset = j - entries // 2
        peers["term", offset] = (others[j], after(offset, True), j, entries - 1 - j, j)
    peers["edge", -1] = (below, after(-1, False), 0, 1, entries)
    peers["edge", 1] = (above, after(1, False), 1, 0, entries + 1)
    order = [("term", 0), ("edge", 1), ("term", 1), ("term", 2), ("edge", -1), ("term", -2), ("term", -1)]

    sends = [("term", 1), ("term", 2), ("term", -2), ("term", -1), ("term", 0), ("edge", 1), ("edge", -1)]
    barrier = pltpu.get_barrier_semaphore()
    before = 0
    for key in order:
        device, is_after = peers[key][:2]

        @pl.when(is_after)
        def _(device=device):
            pl.semaphore_signal(barrier, inc=1, device_id=device, device_id_type=MESH)

        before = before + jnp.where(is_after, 0, 1)

    @pl.when(before > 0)
    def _():
        pl.semaphore_wait(barrier, before)

    for key in sends:
        device, is_after, _, _, number = peers[key]

        @pl.when(jnp.logical_not(is_after))
        def _(device=device, number=number):
            pl.semaphore_signal(ready.at[number], inc=1, device_id=device, device_id_type=MESH)

    for copy in early:
        copy.wait()
    flux = [
        force[i * rows:(i + 1) * rows, :] + gain_s[0, i] * surface[(i % nvars) * rows:(i % nvars + 1) * rows, :]
        for i in range(nf)
    ]
    head = [x.astype(jnp.bfloat16) for x in flux]
    tail = [(x - y.astype(jnp.float32)).astype(jnp.bfloat16) for x, y in zip(flux, head, strict=True)]
    both = jnp.concatenate([jnp.concatenate(head, axis=0), jnp.concatenate(tail, axis=0)], axis=1)
    def to(key):
        device, _, out_slot = peers[key][:3]
        here, there, done, came = (
            (term_out, term_in, term_send, term_recv) if key[0] == "term" else (edge_out, edge_in, edge_send, edge_recv)
        )
        return pltpu.make_async_remote_copy(
            src_ref=here.at[out_slot], dst_ref=there.at[out_slot], send_sem=done.at[out_slot], recv_sem=came.at[out_slot],
            device_id=device, device_id_type=MESH,
        )

    def arrived(key):
        slot_in = peers[key][3]
        there, done, came = (term_in, term_send, term_recv) if key[0] == "term" else (edge_in, edge_send, edge_recv)
        pltpu.make_async_remote_copy(
            src_ref=there.at[slot_in], dst_ref=there.at[slot_in], send_sem=done.at[slot_in], recv_sem=came.at[slot_in],
            device_id=peers[key][0], device_id_type=MESH,
        ).wait_recv()

    slot = lax.broadcasted_iota(jnp.int32, (1, slots), 1)
    def compute(j):
        index = src_v[j]
        column = one_hot(index & (cols - 1), cols).astype(jnp.bfloat16)
        weight = jnp.where(slot < count_s[0, j], inter_v[j], 0.0)
        pick = one_hot(index >> shift, rows) * weight
        found = jnp.dot(both, jnp.concatenate([column, column], axis=0), preferred_element_type=jnp.float32)
        picked = jnp.sum(found.reshape(nf, rows, slots) * pick[None], axis=1)
        term_out[j, :, :] = jnp.concatenate(
            [picked, jnp.zeros((term_out.shape[1] - nf, slots), jnp.float32)], axis=0
        ).astype(jnp.bfloat16)

    def leave(group):
        for key in group:
            compute(peers[key][2])
        for key in group:

            @pl.when(jnp.logical_not(peers[key][1]))
            def _(key=key):
                to(key).start()

    leave(sends[:2])
    for copy in middle:
        copy.wait()
    for side, (near, far) in enumerate(((0, 1), (rows - 1, rows - 2))):
        edge_out[side, 0:levels, :] = wide(field, pl.ds(near, levels, stride=rows)).astype(jnp.bfloat16)
        edge_out[side, levels:2 * levels, :] = wide(field, pl.ds(far, levels, stride=rows)).astype(jnp.bfloat16)
        edge_out[side, 2 * levels:, :] = jnp.broadcast_to(coef[near:near + 1, :], (16, cols)).astype(jnp.bfloat16)

    for key in sends[entries:]:

        @pl.when(jnp.logical_not(peers[key][1]))
        def _(key=key):
            to(key).start()

    leave(sends[2:entries])

    row = lax.broadcasted_iota(jnp.int32, (GROUP, 8, cols), 1)
    first, last = row == 0, row == 7
    halves = (coef[0:8, :][None], coef[8:16, :][None])

    def group(i, carry):
        at = pl.multiple_of(i * (GROUP * rows), GROUP * rows)
        block = wide(field, pl.ds(at, GROUP * rows)).reshape(GROUP, rows, cols)
        low, high = block[:, 0:8], block[:, 8:16]
        low, high = interior_step(low, high, halves, first, last)
        low, high = interior_step(low, high, halves, first, last)
        put(result, pl.ds(at, GROUP * rows), jnp.concatenate([low, high], axis=1).reshape(GROUP * rows, cols))
        return carry

    lax.fori_loop(0, levels // GROUP, group, 0)

    for copy in late:
        copy.wait()
    for j in range(entries):
        spread[j * slots:(j + 1) * slots, :] = one_hot(dst_v[j] & (cols - 1), cols).T.astype(jnp.bfloat16)
        masks[j, :, :] = one_hot(dst_v[j] >> shift, rows)
    inverse[...] = 1.0 / cell[...]

    near = [("term", -2), ("term", -1), ("edge", -1), ("edge", 1), ("term", 0), ("term", 1), ("term", 2)]
    for wraps, keys in ((False, near), (True, [("edge", -1), ("term", -2), ("term", -1)])):
        for key in keys:
            kind, offset = key
            due = peers[key][1]
            if offset < 0:
                under = z + offset < 0
                due = jnp.logical_and(due, under if wraps else jnp.logical_not(under))

            @pl.when(due)
            def _(key=key, kind=kind, offset=offset):
                pl.semaphore_wait(ready.at[peers[kind, -offset][4]], 1)
                to(key).start()

    for side, (near, far) in ((0, (rows - 1, rows - 2)), (1, (0, 1))):
        arrived(("edge", 1 if side == 0 else -1))
        k_near, k_far = coef[near:near + 1, :], coef[far:far + 1, :]
        k_out = edge_in[side, 2 * levels:, :].astype(jnp.float32)[0:1, :]
        for g in range(0, levels, SLAB):
            h = edge_in[side, g:g + SLAB, :].astype(jnp.float32)
            h2 = edge_in[side, levels + g:levels + g + SLAB, :].astype(jnp.float32)
            at_near = pl.ds(near + g * rows, SLAB, stride=rows)
            at_far = pl.ds(far + g * rows, SLAB, stride=rows)
            a = h + k_out * (h2 + sides(h) - 4.0 * h + wide(field, at_near))
            b = k_near * h
            put(result, at_near, wide(result, at_near) + (b + k_near * (a + sides(b) - 4.0 * b)))
            put(result, at_far, wide(result, at_far) + k_far * b)
    for key in order:
        if key[0] == "term":
            arrived(key)
    for key in order:
        to(key).wait_send()


def finish_kernel(nvars, nf, entries, slots, result, term_in, spread, masks, inverse, out, rem, total, store_sem):
    lanes = result.shape[2]
    rows, cols = inverse.shape
    stores = [
        pltpu.make_async_copy(result.at[h], out.at[:, pl.ds(h * lanes, lanes)], store_sem.at[h]) for h in range(2)
    ]
    for copy in stores:
        copy.start()
    placed = []
    for j in range(entries):
        value = term_in[j].astype(jnp.float32)
        here = masks[j]
        placed.append(jnp.concatenate([value[i:i + 1, :] * here for i in range(nf)], axis=0).astype(jnp.bfloat16))
    acc = jnp.dot(jnp.concatenate(placed, axis=1), spread[...], preferred_element_type=jnp.float32)
    scale = inverse[...]
    for i in range(nf):
        total[i * rows:(i + 1) * rows, :] = acc[i * rows:(i + 1) * rows, :] * scale
    stores.append(pltpu.make_async_copy(total, rem, store_sem.at[2]))
    stores[-1].start()
    for copy in stores:
        copy.wait()


def local(state, kappa, forcing, flux_gain, src_index, intersection, pair_count, dst_index, cell_area):
    _, nvars, deep, rows, cols = state.shape
    nf = forcing.shape[1]
    entries, slots = src_index.shape[2:]
    levels = nvars * deep
    n_comp, n_tile = lax.axis_size("comp"), lax.axis_size("tile")
    hbm = pl.BlockSpec(memory_space=pl.ANY)
    pad = -(-nf // 16) * 16
    f32, bf16, i32 = jnp.float32, jnp.bfloat16, jnp.int32
    dma = pltpu.SemaphoreType.DMA
    n_loads = nvars + 8 + 2 * CHUNKS
    vmem = pl.BlockSpec(memory_space=pltpu.VMEM)
    passed = pl.pallas_call(
        functools.partial(kernel, n_comp, n_tile, nvars, nf, entries, slots),
        out_shape=(
            pltpu.VMEM((2, levels * rows, cols // 2), f32),
            pltpu.VMEM((entries, pad, slots), bf16),
            pltpu.VMEM((entries * slots, cols), bf16),
            pltpu.VMEM((entries, rows, slots), f32),
            pltpu.VMEM((rows, cols), f32),
        ),
        in_specs=[hbm] * 9,
        out_specs=(vmem,) * 5,
        scratch_shapes=[
            pltpu.VMEM((2, levels * rows, cols // 2), f32),
            pltpu.VMEM((nvars * rows, cols), f32),
            pltpu.VMEM((nf * rows, cols), f32),
            pltpu.VMEM((rows, cols), f32),
            pltpu.VMEM((rows, cols), f32),
            pltpu.VMEM((entries, 1, slots), i32),
            pltpu.VMEM((entries, 1, slots), f32),
            pltpu.VMEM((entries, 1, slots), i32),
            pltpu.SMEM((1, nf), f32),
            pltpu.SMEM((1, entries), i32),
            pltpu.VMEM((2, 2 * levels + 16, cols), bf16),
            pltpu.VMEM((2, 2 * levels + 16, cols), bf16),
            pltpu.VMEM((entries, pad, slots), bf16),
            pltpu.SemaphoreType.REGULAR((entries + 2,)),
            dma((n_loads,)),
            dma((2,)),
            dma((2,)),
            dma((entries,)),
            dma((entries,)),
        ],
        compiler_params=pltpu.CompilerParams(
            collective_id=0, has_side_effects=True, vmem_limit_bytes=LIMIT
        ),
        cost_estimate=pl.CostEstimate(flops=10**8, bytes_accessed=4 * 10**6, transcendentals=0),
    )(
        *[
            pltpu.with_memory_space_constraint(x, pltpu.HBM)
            for x in (
                state.reshape(levels * rows, cols),
                kappa[0],
                forcing.reshape(nf * rows, cols),
                flux_gain,
                src_index.reshape(entries, 1, slots),
                intersection.reshape(entries, 1, slots),
                pair_count.reshape(1, entries),
                dst_index.reshape(entries, 1, slots),
                cell_area[0],
            )
        ]
    )
    out, rem = pl.pallas_call(
        functools.partial(finish_kernel, nvars, nf, entries, slots),
        out_shape=(
            jax.ShapeDtypeStruct((levels * rows, cols), f32),
            jax.ShapeDtypeStruct((nf * rows, cols), f32),
        ),
        in_specs=[vmem] * 5,
        out_specs=(hbm, hbm),
        scratch_shapes=[pltpu.VMEM((nf * rows, cols), f32), dma((3,))],
        compiler_params=pltpu.CompilerParams(vmem_limit_bytes=LIMIT),
        cost_estimate=pl.CostEstimate(flops=10**8, bytes_accessed=4 * 10**6, transcendentals=0),
    )(*passed)
    return out.reshape(1, nvars, deep, rows, cols), rem.reshape(1, nf, rows, cols)


def solution(mesh):
    return jax.shard_map(
        local,
        mesh=mesh,
        in_specs=(
            P("comp", None, None, "tile", None),
            P("comp", "tile", None),
            P("comp", None, "tile", None),
            P("comp", None),
            P("comp", "tile", None, None),
            P("comp", "tile", None, None),
            P("comp", "tile", None),
            P("comp", "tile", None, None),
            P("comp", "tile", None),
        ),
        out_specs=(P("comp", None, None, "tile", None), P("comp", None, "tile", None)),
        check_vma=False,
    )
```
